32 devices in a mesh: groups: 2 (over y), shot: 4 (over x, core), slab: 4 (over z).
Axes of the slice: x: 2, y: 2, z: 4, core: 2. Of those that a mesh axis runs over, the one named last changes fastest.
Arguments:
- slowness: float32 [32, 192, 128], P(('groups', 'slab')), parts along dimension 0, may hold values from 0.8 to 1.25
- wave_prev: float32 [8, 16, 192, 128], P(('groups', 'shot'), 'slab'), parts along dimension 0, may hold values from -6 to 6
- wave_now: float32 [8, 16, 192, 128], P(('groups', 'shot'), 'slab'), parts along dimension 0, may hold values from -6 to 6
- memory: float32 [8, 3, 16, 192, 128], P(('groups', 'shot'), None, 'slab'), parts along dimension 0, may hold values from -6 to 6
- adjoint_now: float32 [8, 16, 192, 128], P(('groups', 'shot'), 'slab'), parts along dimension 0, may hold values from -6 to 6
- adjoint_prev: float32 [8, 16, 192, 128], P(('groups', 'shot'), 'slab'), parts along dimension 0, may hold values from -6 to 6
- wavelet: float32 [4], replicated, may hold values from -16 to 16
- src_cells: int32 [8, 64], P(('groups', 'shot')), parts along dimension 0, may hold values from 0 to 393215
- src_signs: int32 [8, 64], P(('groups', 'shot')), parts along dimension 0, may hold values from -1 to 1, as said below
- rec_cells: int32 [512], P('groups'), parts along dimension 0, may hold values from 0 to 393215
- observed: float32 [8, 4, 256], P(('groups', 'shot')), parts along dimension 0, may hold values from -6 to 6
Outputs:
- new_slowness: float32 [32, 192, 128], P(('groups', 'slab')), parts along dimension 0
- gradient: float32 [32, 192, 128], P(('groups', 'slab'), 'shot'), parts along dimension 0
The draws below stay inside these ranges and needn't reach their ends.
There are 2 independent parts, one for each index of `groups`. The reference program is written for one: setup_inputs(seed, part) draws one part's arguments, and reference() takes and returns one part's arrays. A program takes and returns all parts, laid end to end along the dimension named above; an argument that names none is the same for every part. Nothing has to cross between parts.
Inputs may be any that keep to these rules, and one draw needn't show every extreme that they name: `src_signs`: each entry is -1 or +1.
All inputs are finite; a program needn't handle non-finite values.
Results may differ from the reference program's by a relative error of at most 0.0001.
Values sent between devices are 32-bit elements; how exact they have to be, the bound alone decides.
A program may use at most 64 MiB of HBM per device.

```python
import jax
import jax.numpy as jnp
from jax import lax

NX = 192
NY = 128
STEPS = 4
NMECH = 3
NSRC = 64
NREC = 256
SHOTS = 4
NZ = 16


def draw_src_signs(key, part):
    picked = jax.random.randint(key, (SHOTS, NSRC), 0, 2)
    signs = 2 * picked - 1
    signs = signs.at[:, 0].set(1).at[:, 1].set(-1)
    return signs.astype(jnp.int32)


def set_ends(values, stream_key, low, high):
    index_at = [jax.random.randint(jax.random.fold_in(stream_key, axis), (), 0, length) for axis, length in enumerate(values.shape)]
    longest = values.shape.index(max(values.shape))
    beside = index_at[:longest] + [(index_at[longest] + 1) % values.shape[longest]] + index_at[longest + 1:]
    return values.at[tuple(index_at)].set(low).at[tuple(beside)].set(high)


def shard_levels(stream_key, extent, shards, least, top_value):
    gain, own = 1.0, jax.random.fold_in(stream_key, 6)
    for position, shards_of in shards:
        heights = jnp.exp(jax.random.uniform(jax.random.fold_in(own, position), (shards_of,), jnp.float32, least / len(shards), top_value / len(shards)))
        gain = gain * jnp.repeat(heights, extent[position] // shards_of).reshape([-1 if axis == position else 1 for axis in range(len(extent))])
    return gain


def gaussian(own_key, dims, spread, most, split=(), held_as=jnp.bfloat16):
    level = shard_levels(own_key, dims, split, -0.22, 0.18) if split else 1.0
    result = jax.random.normal(own_key, dims, jnp.float32) * spread * level
    return jnp.minimum(jnp.maximum(result, -most), most).astype(held_as)


def setup_inputs(seed: int = 0, part: int = 0) -> dict:
    keys = jax.random.split(jax.random.key(seed), 12)
    part_keys = jax.random.split(jax.random.fold_in(keys[11], part), 12)
    return {
        "slowness": jnp.clip(0.8 + 0.45 * jax.random.uniform(part_keys[0], (NZ, NX, NY), jnp.float32) ** shard_levels(part_keys[0], (NZ, NX, NY), ((0, 4),), -0.2, 0.2), 0.8, 1.25),
        "wave_prev": gaussian(part_keys[1], (SHOTS, NZ, NX, NY), 1.0, 6.0, ((0, 4), (1, 4)), jnp.float32),
        "wave_now": gaussian(part_keys[2], (SHOTS, NZ, NX, NY), 1.0, 6.0, ((0, 4), (1, 4)), jnp.float32),
        "memory": gaussian(part_keys[3], (SHOTS, NMECH, NZ, NX, NY), 1.0, 6.0, ((0, 4), (2, 4)), jnp.float32),
        "adjoint_now": gaussian(part_keys[4], (SHOTS, NZ, NX, NY), 1.0, 6.0, ((0, 4), (1, 4)), jnp.float32),
        "adjoint_prev": gaussian(part_keys[5], (SHOTS, NZ, NX, NY), 1.0, 6.0, ((0, 4), (1, 4)), jnp.float32),
        "wavelet": gaussian(keys[6], (STEPS,), 4.0, 16.0, (), jnp.float32),
        "src_cells": set_ends(jax.random.randint(part_keys[7], (SHOTS, NSRC), 0, NZ * NX * NY), jax.random.fold_in(part_keys[7], 1), 0, (NZ * NX * NY) - 1).astype(jnp.int32),
        "src_signs": draw_src_signs(jax.random.fold_in(jax.random.fold_in(keys[11], part), 71), part),
        "rec_cells": set_ends(jax.random.randint(part_keys[9], (NREC,), 0, NZ * NX * NY), jax.random.fold_in(part_keys[9], 1), 0, (NZ * NX * NY) - 1).astype(jnp.int32),
        "observed": gaussian(part_keys[10], (SHOTS, STEPS, NREC), 1.0, 6.0, ((0, 4),), jnp.float32),
    }


center_coef = -2.5
near_coef = 4.0 / 3.0
far_coef = -1.0 / 12.0
courant = 0.14
relax_decay = (0.3, 0.7, 0.95)
relax_weight = (0.3, 0.2, 0.1)
update_rate = 0.05
tiny_eps = 1e-06

def laplace(padded):
    middle = padded[2:-2]
    flanks = jnp.pad(middle, ((0, 0), (2, 2), (2, 2)))
    depth_sum = near_coef * (padded[3:-1] + padded[1:-3]) + far_coef * (padded[4:] + padded[:-4])
    cross_sum = near_coef * (flanks[:, 3:-1, 2:-2] + flanks[:, 1:-3, 2:-2]) + far_coef * (flanks[:, 4:, 2:-2] + flanks[:, :-4, 2:-2])
    along_sum = near_coef * (flanks[:, 2:-2, 3:-1] + flanks[:, 2:-2, 1:-3]) + far_coef * (flanks[:, 2:-2, 4:] + flanks[:, 2:-2, :-4])
    return 3.0 * center_coef * middle + depth_sum + cross_sum + along_sum

def forward_shot(slowness, older, current, relax, src_field, wavelet, rec_cells):
    decay = jnp.array(relax_decay, jnp.float32)[:, None, None, None]
    weight = jnp.array(relax_weight, jnp.float32)[:, None, None, None]
    scaled = courant / (slowness * slowness)
    traces = []
    for level in range(STEPS):
        curved = laplace(jnp.pad(current, ((2, 2), (0, 0), (0, 0))))
        accel = curved + lax.optimization_barrier(jnp.sum(relax, 0))
        newer = 2.0 * current - older + scaled * accel + wavelet[level] * src_field
        relax = decay * relax - weight * curved[None]
        older, current = (current, newer)
        traces.append(current.reshape(-1)[rec_cells])
    return (jnp.stack(traces), current, older)

def reference(slowness, wave_prev, wave_now, memory, adjoint_now, adjoint_prev, wavelet, src_cells, src_signs, rec_cells, observed):

    def per_shot(total, items):
        older, current, relax, back_now, back_prev, cells, signs, seen = items
        src_field = jnp.zeros((NZ * NX * NY,), jnp.float32).at[cells].add(signs.astype(jnp.float32)).reshape(NZ, NX, NY)

        def model_map(model):
            return forward_shot(model, older, current, relax, src_field, wavelet, rec_cells)
        outputs, pullback = jax.vjp(model_map, slowness)
        grad_s, = pullback((outputs[0] - seen, back_now, back_prev))
        return (total + grad_s, None)
    start = jnp.zeros((NZ, NX, NY), jnp.float32)
    total, _ = lax.scan(per_shot, start, (wave_prev, wave_now, memory, adjoint_now, adjoint_prev, src_cells, src_signs, observed))
    squares = jnp.sum(total * total)
    rms_value = jnp.sqrt(squares / (NZ * NX * NY) + tiny_eps)
    gradient = total / rms_value
    new_slowness = slowness - update_rate * gradient
    return (new_slowness, gradient)
```

```python
import functools

import jax
import jax.numpy as jnp
from jax import lax
from jax.experimental import pallas as pl
from jax.experimental.pallas import tpu as pltpu
from jax.sharding import PartitionSpec as P

STEPS = 4
MECH = 3
LINK = 2
PAD = 8
CHUNKS = 4
SUB = 24

center_coef = -2.5
near_coef = 4.0 / 3.0
far_coef = -1.0 / 12.0
courant = 0.14
relax_decay = (0.3, 0.7, 0.95)
relax_weight = (0.3, 0.2, 0.1)
update_rate = 0.05
tiny_eps = 1e-06

MESH = pl.DeviceIdType.MESH


def contract_lanes(a, b):
    return lax.dot_general(a, b, (((1,), (1,)), ((), ())), preferred_element_type=jnp.float32)


def kernel(
    shots,
    slabs,
    slowness_in,
    prev_in,
    now_in,
    memory_in,
    adj_now_in,
    adj_prev_in,
    wavelet,
    src_cells,
    src_signs,
    rec_cells,
    observed,
    total_out,
    inv_out,
    slow,
    older,
    field,
    relax,
    adj_now,
    adj_prev,
    drive,
    united,
    saved,
    back_relax,
    accum,
    scaled,
    factor,
    count,
    seen,
    source,
    pieces,
    halo,
    grad,
    parts,
    total,
    squares,
    load_sem,
    halo_send,
    halo_recv,
    part_send,
    part_recv,
    whole_send,
    whole_recv,
    square_send,
    square_recv,
):
    depth, width, lanes = slow.shape
    rows = width // CHUNKS
    stages = 2 * STEPS - 1
    me = lax.axis_index("slab")
    shot = lax.axis_index("shot")

    loads = [
        pltpu.make_async_copy(now_in.at[0], field.at[0, :, PAD : PAD + width], load_sem.at[0]),
        pltpu.make_async_copy(slowness_in, slow, load_sem.at[1]),
        pltpu.make_async_copy(memory_in.at[0], relax, load_sem.at[2]),
        pltpu.make_async_copy(prev_in.at[0], older, load_sem.at[3]),
        pltpu.make_async_copy(adj_now_in.at[0], adj_now, load_sem.at[4]),
        pltpu.make_async_copy(adj_prev_in.at[0], adj_prev, load_sem.at[5]),
    ]
    barrier = pltpu.get_barrier_semaphore()
    for k in range(1, slabs):
        pl.semaphore_signal(
            barrier, inc=1, device_id={"slab": lax.rem(me + k, slabs)}, device_id_type=MESH
        )
    for k in range(1, shots):
        pl.semaphore_signal(
            barrier, inc=1, device_id={"shot": lax.rem(shot + k, shots)}, device_id_type=MESH
        )
    for copy in loads:
        copy.start()
    pl.semaphore_wait(barrier, slabs - 1 + shots - 1)

    def outgoing(stage, side, c):
        first = depth - LINK if side == 0 else 0
        planes = pl.ds(first, LINK)
        start = pl.multiple_of(c * rows, 8)
        if stage == 0:
            src = now_in.at[0, planes, pl.ds(start, rows)]
        elif stage < STEPS:
            src = field.at[stage, planes, pl.ds(start + PAD, rows)]
        else:
            src = drive.at[stage - STEPS, planes, pl.ds(start + PAD, rows)]
        target = me + 1 if side == 0 else me - 1
        return pltpu.make_async_remote_copy(
            src_ref=src,
            dst_ref=halo.at[stage, side, :, pl.ds(start, rows)],
            send_sem=halo_send.at[stage, side, c],
            recv_sem=halo_recv.at[stage, side, c],
            device_id={"slab": target},
            device_id_type=MESH,
        )

    has_up = me < slabs - 1
    has_down = me > 0

    def send_halo(stage, c):
        @pl.when(has_up)
        def _():
            outgoing(stage, 0, c).start()

        @pl.when(has_down)
        def _():
            outgoing(stage, 1, c).start()

    def wait_sent(stage, c):
        @pl.when(has_up)
        def _():
            outgoing(stage, 0, c).wait_send()

        @pl.when(has_down)
        def _():
            outgoing(stage, 1, c).wait_send()

    def wait_halo(stage, c):
        @pl.when(has_down)
        def _():
            outgoing(stage, 0, c).wait_recv()

        @pl.when(has_up)
        def _():
            outgoing(stage, 1, c).wait_recv()

    for c in range(CHUNKS):
        send_halo(0, c)

    @pl.when(jnp.logical_not(has_down))
    def _():
        halo[:, 0] = jnp.zeros((stages, LINK, width, lanes), jnp.float32)

    @pl.when(jnp.logical_not(has_up))
    def _():
        halo[:, 1] = jnp.zeros((stages, LINK, width, lanes), jnp.float32)

    edge = jnp.zeros((depth, PAD, lanes), jnp.float32)
    for n in range(STEPS):
        field[n, :, :PAD] = edge
        field[n, :, PAD + width :] = edge
    for n in range(STEPS - 1):
        drive[n, :, :PAD] = edge
        drive[n, :, PAD + width :] = edge

    def one_hot(index, height):
        at = lax.broadcasted_iota(jnp.int32, (height, index.shape[1]), 0)
        return jnp.where(at == index, 1.0, 0.0)

    first_row = me * (depth * width)
    rec = rec_cells[...]
    rec_row = lax.div(rec, lanes)
    rec_lane = rec - rec_row * lanes
    rec_row = rec_row - first_row
    at_lane = one_hot(rec_lane, lanes)
    pieces[0:lanes] = at_lane.astype(jnp.bfloat16)
    for n in range(STEPS):
        rest = at_lane * observed[0, n : n + 1, :]
        for k in range(3):
            part = rest.astype(jnp.bfloat16)
            begin = (1 + 3 * n + k) * lanes
            pieces[begin : begin + lanes] = part
            rest = rest - part.astype(jnp.float32)
    src = src_cells[...]
    src_row = lax.div(src, lanes)
    src_lane = src - src_row * lanes
    src_row = src_row - first_row
    src_at = (one_hot(src_lane, lanes) * src_signs[...].astype(jnp.float32)).astype(jnp.bfloat16)
    for d in range(depth):
        at_row = one_hot(rec_row - d * width, width).astype(jnp.bfloat16)
        count[d] = contract_lanes(at_row, pieces[0:lanes])
        for n in range(STEPS):
            begin = (1 + 3 * n) * lanes
            got = contract_lanes(at_row, pieces[begin : begin + 3 * lanes])
            seen[n, d] = (
                got[:, 2 * lanes :] + got[:, lanes : 2 * lanes]
            ) + got[:, :lanes]
        src_rows = one_hot(src_row - d * width, width).astype(jnp.bfloat16)
        source[d] = contract_lanes(src_rows, src_at)

    loads[1].wait()
    for d in range(depth):
        s = slow[d]
        held = courant / (s * s)
        scaled[d] = held
        factor[d] = (-2.0 * held) / s
    for k in (0, 2, 3, 4, 5):
        loads[k].wait()

    lane = lax.broadcasted_iota(jnp.int32, (8, lanes), 1)[:1]
    left_1 = jnp.where(lane >= 1, near_coef, 0.0)
    left_2 = jnp.where(lane >= 2, far_coef, 0.0)
    right_1 = jnp.where(lane < lanes - 1, near_coef, 0.0)
    right_2 = jnp.where(lane < lanes - 2, far_coef, 0.0)

    def laplace(ref, n, stage, d, r):
        def plane(q):
            if q < 0:
                return halo[stage, 0, q + LINK, pl.ds(r, SUB)]
            if q >= depth:
                return halo[stage, 1, q - depth, pl.ds(r, SUB)]
            return ref[n, q, pl.ds(r + PAD, SUB)]

        mid = ref[n, d, pl.ds(r + PAD, SUB)]
        near = (plane(d - 1) + plane(d + 1)) + (
            ref[n, d, pl.ds(r + PAD - 1, SUB)] + ref[n, d, pl.ds(r + PAD + 1, SUB)]
        )
        far = (plane(d - 2) + plane(d + 2)) + (
            ref[n, d, pl.ds(r + PAD - 2, SUB)] + ref[n, d, pl.ds(r + PAD + 2, SUB)]
        )
        along = (
            left_1 * pltpu.roll(mid, 1, 1)
            + right_1 * pltpu.roll(mid, lanes - 1, 1)
            + left_2 * pltpu.roll(mid, 2, 1)
            + right_2 * pltpu.roll(mid, lanes - 2, 1)
        )
        return (3.0 * center_coef) * mid + near_coef * near + far_coef * far + along, mid

    def blocks(c, body):
        for d in range(depth):
            for k in range(rows // SUB):
                body(d, pl.multiple_of(c * rows + k * SUB, 8))

    def adjoint_part(level, d, r, back, begin_accum):
        at = pl.ds(r, SUB)
        up = back + (
            count[d, at] * field[level + 1, d, pl.ds(r + PAD, SUB)] - seen[level, d, at]
        )
        term = up * saved[level, d, at]
        term = term if begin_accum else accum[d, at] + term
        if level == 0:
            grad[d, at] = term * factor[d, at]
            return
        accum[d, at] = term
        united[level, d, at] = up
        pushed = scaled[d, at] * up
        out = pushed
        for m in range(MECH):
            if begin_accum:
                back_relax[m, d, at] = pushed
            else:
                held = back_relax[m, d, at]
                out = out - relax_weight[m] * held
                if level > 1:
                    back_relax[m, d, at] = relax_decay[m] * held + pushed
        drive[STEPS - 1 - level, d, pl.ds(r + PAD, SUB)] = out

    def forward_stage(n):
        amount = wavelet[n]

        def chunk(c, carry):
            wait_halo(n, c)
            if n > 0:
                wait_sent(n - 1, c)

            def body(d, r):
                at = pl.ds(r, SUB)
                inner = pl.ds(r + PAD, SUB)
                curved, mid = laplace(field, n, n, d, r)
                held = [relax[m, d, at] for m in range(MECH)]
                accel = curved + ((held[0] + held[1]) + held[2])
                before = older[d, at] if n == 0 else field[n - 1, d, inner]
                saved[n, d, at] = accel
                field[n + 1, d, inner] = (
                    (2.0 * mid - before) + scaled[d, at] * accel + amount * source[d, at]
                )
                if n < STEPS - 1:
                    for m in range(MECH):
                        relax[m, d, at] = relax_decay[m] * held[m] - relax_weight[m] * curved
                else:
                    adjoint_part(STEPS - 1, d, r, adj_now[d, at], True)

            blocks(c, body)
            send_halo(n + 1, c)
            return carry

        lax.fori_loop(0, CHUNKS, chunk, 0)

    piece = depth * rows // shots

    def spot(owner, c):
        begin = owner * piece
        return begin // rows, pl.multiple_of(c * rows + begin % rows, 8)

    def part_copy(k, c):
        target = lax.rem(shot + k, shots)
        d, r = spot(target, c)
        return pltpu.make_async_remote_copy(
            src_ref=grad.at[d, pl.ds(r, piece)],
            dst_ref=parts.at[c, k - 1],
            send_sem=part_send.at[c, k - 1],
            recv_sem=part_recv.at[c, k - 1],
            device_id={"shot": target},
            device_id_type=MESH,
        )

    def whole_copy(k, c):
        target = lax.rem(shot + k, shots)
        d, r = spot(shot, c)
        return pltpu.make_async_remote_copy(
            src_ref=total.at[d, pl.ds(r, piece)],
            dst_ref=total.at[d, pl.ds(r, piece)],
            send_sem=whole_send.at[c, k - 1],
            recv_sem=whole_recv.at[c, k - 1],
            device_id={"shot": target},
            device_id_type=MESH,
        )

    def reduce_chunk(c):
        d, r = spot(shot, c)
        held = grad[d, pl.ds(r, piece)]
        for k in range(1, shots):
            part_copy(k, c).wait_recv()
            held = held + parts[c, k - 1]
        total[d, pl.ds(r, piece)] = held
        for k in range(1, shots):
            whole_copy(k, c).start()

    def backward_stage(level):
        stage = 2 * STEPS - 2 - level

        def chunk(c, carry):
            wait_halo(stage, c)
            wait_sent(stage - 1, c)

            def body(d, r):
                at = pl.ds(r, SUB)
                curved, _ = laplace(drive, stage - STEPS, stage, d, r)
                after = united[level + 1, d, at]
                if level == STEPS - 2:
                    base = adj_prev[d, at]
                else:
                    base = -united[level + 2, d, at]
                adjoint_part(level, d, r, (base + 2.0 * after) + curved, False)

            blocks(c, body)
            if level > 0:
                send_halo(stage + 1, c)
            else:
                for k in range(1, shots):
                    part_copy(k, c).start()

                @pl.when(c >= 2)
                def _():
                    reduce_chunk(c - 2)

            return carry

        lax.fori_loop(0, CHUNKS, chunk, 0)

    for n in range(STEPS):
        forward_stage(n)
    for level in reversed(range(STEPS - 1)):
        backward_stage(level)
    for c in range(CHUNKS - 2, CHUNKS):
        reduce_chunk(c)

    def settle(c, carry):
        wait_sent(stages - 1, c)
        for k in range(1, shots):
            part_copy(k, c).wait_send()
            whole_copy(k, c).wait()
        return carry

    lax.fori_loop(0, CHUNKS, settle, 0)

    store = pltpu.make_async_copy(total, total_out, load_sem.at[0])
    store.start()

    summed = jnp.zeros((8, lanes), jnp.float32)
    for d in range(depth):
        block = total[d]
        summed = summed + jnp.sum((block * block).reshape(width // 8, 8, lanes), axis=0)
    squares[me] = summed

    def square_copy(k):
        return pltpu.make_async_remote_copy(
            src_ref=squares.at[me],
            dst_ref=squares.at[me],
            send_sem=square_send.at[k - 1],
            recv_sem=square_recv.at[k - 1],
            device_id={"slab": lax.rem(me + k, slabs)},
            device_id_type=MESH,
        )

    for k in range(1, slabs):
        square_copy(k).start()
    for k in range(1, slabs):
        square_copy(k).wait()
    everything = squares[0]
    for k in range(1, slabs):
        everything = everything + squares[k]
    cells = slabs * depth * width * lanes
    mean = jnp.sum(everything, keepdims=True) / cells + tiny_eps
    inv_out[...] = jnp.broadcast_to(1.0 / jnp.sqrt(mean), inv_out.shape)
    store.wait()


def per_device(
    slowness,
    wave_prev,
    wave_now,
    memory,
    adjoint_now,
    adjoint_prev,
    wavelet,
    src_cells,
    src_signs,
    rec_cells,
    observed,
):
    depth, width, lanes = slowness.shape
    shots, slabs = lax.axis_size("shot"), lax.axis_size("slab")
    rows = width // CHUNKS
    piece = depth * rows // shots
    assert width % CHUNKS == 0 and rows % SUB == 0 and depth >= LINK
    assert depth * rows % shots == 0 and rows % piece == 0 and piece % 8 == 0
    receivers = rec_cells.shape[0]
    stages = 2 * STEPS - 1
    f32 = jnp.float32
    block = (depth, width, lanes)
    padded = (depth, width + 2 * PAD, lanes)
    anywhere = pl.BlockSpec(memory_space=pl.ANY)
    vmem = pl.BlockSpec(memory_space=pltpu.VMEM)
    smem = pl.BlockSpec(memory_space=pltpu.SMEM)
    dma = pltpu.SemaphoreType.DMA
    total, inverse = pl.pallas_call(
        functools.partial(kernel, shots, slabs),
        name="invert",
        out_shape=(
            jax.ShapeDtypeStruct(block, f32),
            jax.ShapeDtypeStruct((8, lanes), f32),
        ),
        in_specs=[anywhere] * 6 + [smem] + [vmem] * 4,
        out_specs=(anywhere, vmem),
        scratch_shapes=[
            pltpu.VMEM(block, f32),
            pltpu.VMEM(block, f32),
            pltpu.VMEM((STEPS + 1, *padded), f32),
            pltpu.VMEM((MECH, *block), f32),
            pltpu.VMEM(block, f32),
            pltpu.VMEM(block, f32),
            pltpu.VMEM((STEPS - 1, *padded), f32),
            pltpu.VMEM((STEPS, *block), f32),
            pltpu.VMEM((STEPS, *block), f32),
            pltpu.VMEM((MECH, *block), f32),
            pltpu.VMEM(block, f32),
            pltpu.VMEM(block, f32),
            pltpu.VMEM(block, f32),
            pltpu.VMEM(block, f32),
            pltpu.VMEM((STEPS, *block), f32),
            pltpu.VMEM(block, f32),
            pltpu.VMEM(((1 + 3 * STEPS) * lanes, receivers), jnp.bfloat16),
            pltpu.VMEM((stages, 2, LINK, width, lanes), f32),
            pltpu.VMEM(block, f32),
            pltpu.VMEM((CHUNKS, shots - 1, piece, lanes), f32),
            pltpu.VMEM(block, f32),
            pltpu.VMEM((slabs, 8, lanes), f32),
            dma((6,)),
            dma((stages, 2, CHUNKS)),
            dma((stages, 2, CHUNKS)),
            dma((CHUNKS, shots - 1)),
            dma((CHUNKS, shots - 1)),
            dma((CHUNKS, shots - 1)),
            dma((CHUNKS, shots - 1)),
            dma((slabs - 1,)),
            dma((slabs - 1,)),
        ],
        compiler_params=pltpu.CompilerParams(
            collective_id=0, has_side_effects=True, vmem_limit_bytes=40 * 2**20
        ),
    )(
        slowness,
        wave_prev,
        wave_now,
        memory,
        adjoint_now,
        adjoint_prev,
        wavelet,
        src_cells,
        src_signs,
        rec_cells.reshape(1, receivers),
        observed,
    )
    normed = total * inverse[0, 0]
    new_slowness = slowness - update_rate * normed
    share = width // shots
    gradient = lax.dynamic_slice_in_dim(normed, lax.axis_index("shot") * share, share, 1)
    return (new_slowness, gradient)


def solution(mesh):
    in_specs = (
        P(("groups", "slab"), None, None),
        P(("groups", "shot"), "slab", None, None),
        P(("groups", "shot"), "slab", None, None),
        P(("groups", "shot"), None, "slab", None, None),
        P(("groups", "shot"), "slab", None, None),
        P(("groups", "shot"), "slab", None, None),
        P(),
        P(("groups", "shot"), None),
        P(("groups", "shot"), None),
        P("groups"),
        P(("groups", "shot"), None, None),
    )
    out_specs = (P(("groups", "slab"), None, None), P(("groups", "slab"), "shot", None))
    return jax.shard_map(
        per_device, mesh=mesh, in_specs=in_specs, out_specs=out_specs, check_vma=False
    )
```

```python
import functools

import jax
import jax.numpy as jnp
from jax import lax
from jax.experimental import pallas as pl
from jax.experimental.pallas import tpu as pltpu
from jax.sharding import PartitionSpec as P

STEPS = 4
MECH = 3
LINK = 2
PAD = 8
CHUNKS = 4
SUB = 24

center_coef = -2.5
near_coef = 4.0 / 3.0
far_coef = -1.0 / 12.0
courant = 0.14
relax_decay = (0.3, 0.7, 0.95)
relax_weight = (0.3, 0.2, 0.1)
update_rate = 0.05
tiny_eps = 1e-06

MESH = pl.DeviceIdType.MESH


def contract_lanes(a, b):
    return lax.dot_general(a, b, (((1,), (1,)), ((), ())), preferred_element_type=jnp.float32)


def kernel(
    shots,
    slabs,
    slowness_in,
    prev_in,
    now_in,
    memory_in,
    adj_now_in,
    adj_prev_in,
    wavelet,
    src_cells,
    src_signs,
    rec_cells,
    observed,
    total_out,
    inv_out,
    slow,
    older,
    field,
    relax,
    adj_now,
    adj_prev,
    drive,
    united,
    saved,
    back_relax,
    accum,
    scaled,
    factor,
    count,
    seen,
    source,
    hot_rows,
    pieces,
    halo,
    grad,
    parts,
    total,
    squares,
    load_sem,
    halo_send,
    halo_recv,
    part_send,
    part_recv,
    whole_send,
    whole_recv,
    square_send,
    square_recv,
):
    depth, width, lanes = slow.shape
    rows = width // CHUNKS
    stages = 2 * STEPS - 1
    me = lax.axis_index("slab")
    shot = lax.axis_index("shot")

    loads = [
        pltpu.make_async_copy(now_in.at[0], field.at[0, :, PAD : PAD + width], load_sem.at[0]),
        pltpu.make_async_copy(slowness_in, slow, load_sem.at[1]),
        pltpu.make_async_copy(memory_in.at[0], relax, load_sem.at[2]),
        pltpu.make_async_copy(prev_in.at[0], older, load_sem.at[3]),
        pltpu.make_async_copy(adj_now_in.at[0], adj_now, load_sem.at[4]),
        pltpu.make_async_copy(adj_prev_in.at[0], adj_prev, load_sem.at[5]),
    ]
    barrier = pltpu.get_barrier_semaphore()
    for k in range(1, slabs):
        pl.semaphore_signal(
            barrier, inc=1, device_id={"slab": lax.rem(me + k, slabs)}, device_id_type=MESH
        )
    for k in range(1, shots):
        pl.semaphore_signal(
            barrier, inc=1, device_id={"shot": lax.rem(shot + k, shots)}, device_id_type=MESH
        )
    for copy in loads:
        copy.start()
    pl.semaphore_wait(barrier, slabs - 1 + shots - 1)

    def outgoing(stage, side, c):
        first = depth - LINK if side == 0 else 0
        planes = pl.ds(first, LINK)
        start = pl.multiple_of(c * rows, 8)
        if stage == 0:
            src = now_in.at[0, planes, pl.ds(start, rows)]
        elif stage < STEPS:
            src = field.at[stage, planes, pl.ds(start + PAD, rows)]
        else:
            src = drive.at[stage - STEPS, planes, pl.ds(start + PAD, rows)]
        target = me + 1 if side == 0 else me - 1
        return pltpu.make_async_remote_copy(
            src_ref=src,
            dst_ref=halo.at[stage, side, :, pl.ds(start, rows)],
            send_sem=halo_send.at[stage, side, c],
            recv_sem=halo_recv.at[stage, side, c],
            device_id={"slab": target},
            device_id_type=MESH,
        )

    has_up = me < slabs - 1
    has_down = me > 0

    def send_halo(stage, c):
        @pl.when(has_up)
        def _():
            outgoing(stage, 0, c).start()

        @pl.when(has_down)
        def _():
            outgoing(stage, 1, c).start()

    def wait_sent(stage, c):
        @pl.when(has_up)
        def _():
            outgoing(stage, 0, c).wait_send()

        @pl.when(has_down)
        def _():
            outgoing(stage, 1, c).wait_send()

    def wait_halo(stage, c):
        @pl.when(has_down)
        def _():
            outgoing(stage, 0, c).wait_recv()

        @pl.when(has_up)
        def _():
            outgoing(stage, 1, c).wait_recv()

    for c in range(CHUNKS):
        send_halo(0, c)

    @pl.when(jnp.logical_not(has_down))
    def _():
        halo[:, 0] = jnp.zeros((stages, LINK, width, lanes), jnp.float32)

    @pl.when(jnp.logical_not(has_up))
    def _():
        halo[:, 1] = jnp.zeros((stages, LINK, width, lanes), jnp.float32)

    edge = jnp.zeros((depth, PAD, lanes), jnp.float32)
    for n in range(STEPS):
        field[n, :, :PAD] = edge
        field[n, :, PAD + width :] = edge
    for n in range(STEPS - 1):
        drive[n, :, :PAD] = edge
        drive[n, :, PAD + width :] = edge

    def one_hot(index, height):
        at = lax.broadcasted_iota(jnp.int32, (height, index.shape[1]), 0)
        return jnp.where(at == index, 1.0, 0.0)

    first_row = me * (depth * width)
    src = src_cells[...]
    src_row = lax.div(src, lanes)
    src_lane = src - src_row * lanes
    src_at = (one_hot(src_lane, lanes) * src_signs[...].astype(jnp.float32)).astype(jnp.bfloat16)
    src_rows = one_hot(src_row - first_row, depth * width).astype(jnp.bfloat16)
    source[...] = contract_lanes(src_rows, src_at).reshape(depth, width, lanes)

    def place_receivers():
        rec = rec_cells[...]
        rec_row = lax.div(rec, lanes)
        rec_lane = rec - rec_row * lanes
        at_lane = one_hot(rec_lane, lanes)
        pieces[0:lanes] = at_lane.astype(jnp.bfloat16)
        for n in range(STEPS):
            rest = at_lane * observed[0, n : n + 1, :]
            for k in range(3):
                part = rest.astype(jnp.bfloat16)
                begin = (1 + 3 * n + k) * lanes
                pieces[begin : begin + lanes] = part
                rest = rest - part.astype(jnp.float32)
        hot_rows[...] = one_hot(rec_row - first_row, depth * width).astype(jnp.bfloat16)
        count[...] = contract_lanes(hot_rows[...], pieces[0:lanes]).reshape(depth, width, lanes)

    def place_observed(n):
        begin = (1 + 3 * n) * lanes
        got = contract_lanes(hot_rows[...], pieces[begin : begin + 3 * lanes])
        got = (got[:, 2 * lanes :] + got[:, lanes : 2 * lanes]) + got[:, :lanes]
        seen[n] = got.reshape(depth, width, lanes)

    loads[1].wait()
    for d in range(depth):
        s = slow[d]
        held = courant / (s * s)
        scaled[d] = held
        factor[d] = (-2.0 * held) / s
    for k in (0, 2, 3, 4, 5):
        loads[k].wait()

    lane = lax.broadcasted_iota(jnp.int32, (8, lanes), 1)[:1]
    left_1 = jnp.where(lane >= 1, near_coef, 0.0)
    left_2 = jnp.where(lane >= 2, far_coef, 0.0)
    right_1 = jnp.where(lane < lanes - 1, near_coef, 0.0)
    right_2 = jnp.where(lane < lanes - 2, far_coef, 0.0)

    def laplace(ref, n, stage, r):
        def rows_at(d, shift):
            return ref[n, d, pl.ds(r + PAD + shift, SUB)]

        low = [halo[stage, 0, k, pl.ds(r, SUB)] for k in range(LINK)]
        mids = [rows_at(d, 0) for d in range(depth)]
        high = [halo[stage, 1, k, pl.ds(r, SUB)] for k in range(LINK)]
        planes = low + mids + high
        curved = []
        for d in range(depth):
            mid = mids[d]
            near = (planes[d + 1] + planes[d + 3]) + (rows_at(d, -1) + rows_at(d, 1))
            far = (planes[d] + planes[d + 4]) + (rows_at(d, -2) + rows_at(d, 2))
            along = (
                left_1 * pltpu.roll(mid, 1, 1)
                + right_1 * pltpu.roll(mid, lanes - 1, 1)
                + left_2 * pltpu.roll(mid, 2, 1)
                + right_2 * pltpu.roll(mid, lanes - 2, 1)
            )
            curved.append(
                (3.0 * center_coef) * mid + near_coef * near + far_coef * far + along
            )
        return curved, mids

    def blocks(c, body):
        for k in range(rows // SUB):
            body(pl.multiple_of(c * rows + k * SUB, 8))

    def adjoint_part(level, d, r, back, begin_accum):
        at = pl.ds(r, SUB)
        up = back + (
            count[d, at] * field[level + 1, d, pl.ds(r + PAD, SUB)] - seen[level, d, at]
        )
        term = up * saved[level, d, at]
        term = term if begin_accum else accum[d, at] + term
        if level == 0:
            grad[d, at] = term * factor[d, at]
            return
        accum[d, at] = term
        united[level, d, at] = up
        pushed = scaled[d, at] * up
        out = pushed
        for m in range(MECH):
            if begin_accum:
                back_relax[m, d, at] = pushed
            else:
                held = back_relax[m, d, at]
                out = out - relax_weight[m] * held
                if level > 1:
                    back_relax[m, d, at] = relax_decay[m] * held + pushed
        drive[STEPS - 1 - level, d, pl.ds(r + PAD, SUB)] = out

    def forward_stage(n):
        amount = wavelet[n]

        def chunk(c, carry):
            wait_halo(n, c)
            if n > 0:
                wait_sent(n - 1, c)

            def body(r):
                at = pl.ds(r, SUB)
                inner = pl.ds(r + PAD, SUB)
                curved, mids = laplace(field, n, n, r)
                for d in range(depth):
                    held = [relax[m, d, at] for m in range(MECH)]
                    accel = curved[d] + ((held[0] + held[1]) + held[2])
                    before = older[d, at] if n == 0 else field[n - 1, d, inner]
                    newer = (2.0 * mids[d] - before) + scaled[d, at] * accel
                    newer = newer + amount * source[d, at]
                    saved[n, d, at] = accel
                    field[n + 1, d, inner] = newer
                    if n < STEPS - 1:
                        for m in range(MECH):
                            relax[m, d, at] = (
                                relax_decay[m] * held[m] - relax_weight[m] * curved[d]
                            )
                    else:
                        adjoint_part(n, d, r, adj_now[d, at], True)

            blocks(c, body)
            send_halo(n + 1, c)
            return carry

        lax.fori_loop(0, CHUNKS, chunk, 0)

    piece = depth * rows // shots

    def spot(owner, c):
        begin = owner * piece
        return begin // rows, pl.multiple_of(c * rows + begin % rows, 8)

    def part_copy(k, c):
        target = lax.rem(shot + k, shots)
        d, r = spot(target, c)
        return pltpu.make_async_remote_copy(
            src_ref=grad.at[d, pl.ds(r, piece)],
            dst_ref=parts.at[c, k - 1],
            send_sem=part_send.at[c, k - 1],
            recv_sem=part_recv.at[c, k - 1],
            device_id={"shot": target},
            device_id_type=MESH,
        )

    def whole_copy(k, c):
        target = lax.rem(shot + k, shots)
        d, r = spot(shot, c)
        return pltpu.make_async_remote_copy(
            src_ref=total.at[d, pl.ds(r, piece)],
            dst_ref=total.at[d, pl.ds(r, piece)],
            send_sem=whole_send.at[c, k - 1],
            recv_sem=whole_recv.at[c, k - 1],
            device_id={"shot": target},
            device_id_type=MESH,
        )

    def reduce_chunk(c):
        d, r = spot(shot, c)
        held = grad[d, pl.ds(r, piece)]
        for k in range(1, shots):
            part_copy(k, c).wait_recv()
            held = held + parts[c, k - 1]
        total[d, pl.ds(r, piece)] = held
        for k in range(1, shots):
            whole_copy(k, c).start()

    def backward_stage(level):
        stage = 2 * STEPS - 2 - level

        def chunk(c, carry):
            wait_halo(stage, c)
            wait_sent(stage - 1, c)

            def body(r):
                at = pl.ds(r, SUB)
                curved, _ = laplace(drive, stage - STEPS, stage, r)
                for d in range(depth):
                    after = united[level + 1, d, at]
                    if level == STEPS - 2:
                        base = adj_prev[d, at]
                    else:
                        base = -united[level + 2, d, at]
                    adjoint_part(level, d, r, (base + 2.0 * after) + curved[d], False)

            blocks(c, body)
            if level > 0:
                send_halo(stage + 1, c)
            else:
                for k in range(1, shots):
                    part_copy(k, c).start()

                @pl.when(c >= 2)
                def _():
                    reduce_chunk(c - 2)

            return carry

        lax.fori_loop(0, CHUNKS, chunk, 0)

    for n in range(STEPS):
        forward_stage(n)
        if n == 0:
            place_receivers()
        if n in (1, 2):
            for k in (2 * n - 2, 2 * n - 1):
                place_observed(k)
    for level in reversed(range(STEPS - 1)):
        backward_stage(level)
    for c in range(CHUNKS - 2, CHUNKS):
        reduce_chunk(c)

    def settle(c, carry):
        wait_sent(stages - 1, c)
        for k in range(1, shots):
            part_copy(k, c).wait_send()
            whole_copy(k, c).wait()
        return carry

    lax.fori_loop(0, CHUNKS, settle, 0)

    store = pltpu.make_async_copy(total, total_out, load_sem.at[0])
    store.start()

    summed = jnp.zeros((8, lanes), jnp.float32)
    for d in range(depth):
        block = total[d]
        summed = summed + jnp.sum((block * block).reshape(width // 8, 8, lanes), axis=0)
    squares[me] = summed

    def square_copy(k):
        return pltpu.make_async_remote_copy(
            src_ref=squares.at[me],
            dst_ref=squares.at[me],
            send_sem=square_send.at[k - 1],
            recv_sem=square_recv.at[k - 1],
            device_id={"slab": lax.rem(me + k, slabs)},
            device_id_type=MESH,
        )

    for k in range(1, slabs):
        square_copy(k).start()
    for k in range(1, slabs):
        square_copy(k).wait()
    everything = squares[0]
    for k in range(1, slabs):
        everything = everything + squares[k]
    cells = slabs * depth * width * lanes
    mean = jnp.sum(everything, keepdims=True) / cells + tiny_eps
    inv_out[...] = jnp.broadcast_to(1.0 / jnp.sqrt(mean), inv_out.shape)
    store.wait()


def finish(total, slowness, inverse, new_slowness, gradient):
    share = gradient.shape[1]
    first = pl.multiple_of(lax.axis_index("shot") * share, 8)
    inv = inverse[0:1]
    for d in range(total.shape[0]):
        new_slowness[d] = slowness[d] - update_rate * (total[d] * inv)
        gradient[d] = total[d, pl.ds(first, share)] * inv


def per_device(
    slowness,
    wave_prev,
    wave_now,
    memory,
    adjoint_now,
    adjoint_prev,
    wavelet,
    src_cells,
    src_signs,
    rec_cells,
    observed,
):
    depth, width, lanes = slowness.shape
    shots, slabs = lax.axis_size("shot"), lax.axis_size("slab")
    rows = width // CHUNKS
    piece = depth * rows // shots
    assert width % CHUNKS == 0 and rows % SUB == 0 and depth >= LINK
    assert depth * rows % shots == 0 and rows % piece == 0 and piece % 8 == 0
    receivers = rec_cells.shape[0]
    stages = 2 * STEPS - 1
    f32 = jnp.float32
    block = (depth, width, lanes)
    padded = (depth, width + 2 * PAD, lanes)
    anywhere = pl.BlockSpec(memory_space=pl.ANY)
    vmem = pl.BlockSpec(memory_space=pltpu.VMEM)
    smem = pl.BlockSpec(memory_space=pltpu.SMEM)
    dma = pltpu.SemaphoreType.DMA
    total, inverse = pl.pallas_call(
        functools.partial(kernel, shots, slabs),
        name="invert",
        out_shape=(
            jax.ShapeDtypeStruct(block, f32),
            jax.ShapeDtypeStruct((8, lanes), f32),
        ),
        in_specs=[anywhere] * 6 + [smem] + [vmem] * 4,
        out_specs=(anywhere, vmem),
        scratch_shapes=[
            pltpu.VMEM(block, f32),
            pltpu.VMEM(block, f32),
            pltpu.VMEM((STEPS + 1, *padded), f32),
            pltpu.VMEM((MECH, *block), f32),
            pltpu.VMEM(block, f32),
            pltpu.VMEM(block, f32),
            pltpu.VMEM((STEPS - 1, *padded), f32),
            pltpu.VMEM((STEPS, *block), f32),
            pltpu.VMEM((STEPS, *block), f32),
            pltpu.VMEM((MECH, *block), f32),
            pltpu.VMEM(block, f32),
            pltpu.VMEM(block, f32),
            pltpu.VMEM(block, f32),
            pltpu.VMEM(block, f32),
            pltpu.VMEM((STEPS, *block), f32),
            pltpu.VMEM(block, f32),
            pltpu.VMEM((depth * width, receivers), jnp.bfloat16),
            pltpu.VMEM(((1 + 3 * STEPS) * lanes, receivers), jnp.bfloat16),
            pltpu.VMEM((stages, 2, LINK, width, lanes), f32),
            pltpu.VMEM(block, f32),
            pltpu.VMEM((CHUNKS, shots - 1, piece, lanes), f32),
            pltpu.VMEM(block, f32),
            pltpu.VMEM((slabs, 8, lanes), f32),
            dma((6,)),
            dma((stages, 2, CHUNKS)),
            dma((stages, 2, CHUNKS)),
            dma((CHUNKS, shots - 1)),
            dma((CHUNKS, shots - 1)),
            dma((CHUNKS, shots - 1)),
            dma((CHUNKS, shots - 1)),
            dma((slabs - 1,)),
            dma((slabs - 1,)),
        ],
        compiler_params=pltpu.CompilerParams(
            collective_id=0, has_side_effects=True, vmem_limit_bytes=60 * 2**20
        ),
    )(
        slowness,
        wave_prev,
        wave_now,
        memory,
        adjoint_now,
        adjoint_prev,
        wavelet,
        src_cells,
        src_signs,
        rec_cells.reshape(1, receivers),
        observed,
    )
    share = width // shots
    new_slowness, gradient = pl.pallas_call(
        finish,
        name="finish",
        out_shape=(
            jax.ShapeDtypeStruct(block, f32),
            jax.ShapeDtypeStruct((depth, share, lanes), f32),
        ),
        in_specs=[vmem] * 3,
        out_specs=(vmem, vmem),
        compiler_params=pltpu.CompilerParams(vmem_limit_bytes=60 * 2**20),
    )(total, slowness, inverse)
    return (new_slowness, gradient)


def solution(mesh):
    in_specs = (
        P(("groups", "slab"), None, None),
        P(("groups", "shot"), "slab", None, None),
        P(("groups", "shot"), "slab", None, None),
        P(("groups", "shot"), None, "slab", None, None),
        P(("groups", "shot"), "slab", None, None),
        P(("groups", "shot"), "slab", None, None),
        P(),
        P(("groups", "shot"), None),
        P(("groups", "shot"), None),
        P("groups"),
        P(("groups", "shot"), None, None),
    )
    out_specs = (P(("groups", "slab"), None, None), P(("groups", "slab"), "shot", None))
    return jax.shard_map(
        per_device, mesh=mesh, in_specs=in_specs, out_specs=out_specs, check_vma=False
    )
```

```python
import functools

import jax
import jax.numpy as jnp
from jax import lax
from jax.experimental import pallas as pl
from jax.experimental.pallas import tpu as pltpu
from jax.sharding import PartitionSpec as P

STEPS = 4
MECH = 3
LINK = 2
PAD = 8
CHUNKS = 6
SUB = 16

center_coef = -2.5
near_coef = 4.0 / 3.0
far_coef = -1.0 / 12.0
courant = 0.14
relax_decay = (0.3, 0.7, 0.95)
relax_weight = (0.3, 0.2, 0.1)
update_rate = 0.05
tiny_eps = 1e-06

MESH = pl.DeviceIdType.MESH


def contract_lanes(a, b):
    return lax.dot_general(a, b, (((1,), (1,)), ((), ())), preferred_element_type=jnp.float32)


def kernel(
    shots,
    slabs,
    slowness_in,
    prev_in,
    now_in,
    memory_in,
    adj_now_in,
    adj_prev_in,
    wavelet,
    src_cells,
    src_signs,
    rec_cells,
    observed,
    total_out,
    inv_out,
    slow,
    older,
    field,
    relax,
    adj_now,
    adj_prev,
    drive,
    united,
    saved,
    back_relax,
    accum,
    scaled,
    factor,
    count,
    seen,
    source,
    hot_rows,
    pieces,
    halo,
    grad,
    parts,
    total,
    squares,
    load_sem,
    halo_send,
    halo_recv,
    part_send,
    part_recv,
    whole_send,
    whole_recv,
    square_send,
    square_recv,
):
    depth, width, lanes = slow.shape
    rows = width // CHUNKS
    stages = 2 * STEPS - 1
    me = lax.axis_index("slab")
    shot = lax.axis_index("shot")

    loads = [
        pltpu.make_async_copy(now_in.at[0], field.at[0, :, PAD : PAD + width], load_sem.at[0]),
        pltpu.make_async_copy(slowness_in, slow, load_sem.at[1]),
        pltpu.make_async_copy(memory_in.at[0], relax, load_sem.at[2]),
        pltpu.make_async_copy(prev_in.at[0], older, load_sem.at[3]),
        pltpu.make_async_copy(adj_now_in.at[0], adj_now, load_sem.at[4]),
        pltpu.make_async_copy(adj_prev_in.at[0], adj_prev, load_sem.at[5]),
    ]
    barrier = pltpu.get_barrier_semaphore()
    for k in range(1, slabs):
        pl.semaphore_signal(
            barrier, inc=1, device_id={"slab": lax.rem(me + k, slabs)}, device_id_type=MESH
        )
    for k in range(1, shots):
        pl.semaphore_signal(
            barrier, inc=1, device_id={"shot": lax.rem(shot + k, shots)}, device_id_type=MESH
        )
    for copy in loads:
        copy.start()
    pl.semaphore_wait(barrier, slabs - 1 + shots - 1)

    def outgoing(stage, side, c):
        first = depth - LINK if side == 0 else 0
        planes = pl.ds(first, LINK)
        start = pl.multiple_of(c * rows, 8)
        if stage == 0:
            src = now_in.at[0, planes, pl.ds(start, rows)]
        elif stage < STEPS:
            src = field.at[stage, planes, pl.ds(start + PAD, rows)]
        else:
            src = drive.at[stage - STEPS, planes, pl.ds(start + PAD, rows)]
        target = me + 1 if side == 0 else me - 1
        return pltpu.make_async_remote_copy(
            src_ref=src,
            dst_ref=halo.at[stage, side, :, pl.ds(start, rows)],
            send_sem=halo_send.at[stage, side, c],
            recv_sem=halo_recv.at[stage, side, c],
            device_id={"slab": target},
            device_id_type=MESH,
        )

    has_up = me < slabs - 1
    has_down = me > 0

    def send_halo(stage, c):
        @pl.when(has_up)
        def _():
            outgoing(stage, 0, c).start()

        @pl.when(has_down)
        def _():
            outgoing(stage, 1, c).start()

    def wait_sent(stage, c):
        @pl.when(has_up)
        def _():
            outgoing(stage, 0, c).wait_send()

        @pl.when(has_down)
        def _():
            outgoing(stage, 1, c).wait_send()

    def wait_halo(stage, c):
        @pl.when(has_down)
        def _():
            outgoing(stage, 0, c).wait_recv()

        @pl.when(has_up)
        def _():
            outgoing(stage, 1, c).wait_recv()

    for c in range(CHUNKS):
        send_halo(0, c)

    @pl.when(jnp.logical_not(has_down))
    def _():
        halo[:, 0] = jnp.zeros((stages, LINK, width, lanes), jnp.float32)

    @pl.when(jnp.logical_not(has_up))
    def _():
        halo[:, 1] = jnp.zeros((stages, LINK, width, lanes), jnp.float32)

    edge = jnp.zeros((depth, PAD, lanes), jnp.float32)
    for n in range(STEPS):
        field[n, :, :PAD] = edge
        field[n, :, PAD + width :] = edge
    for n in range(STEPS - 1):
        drive[n, :, :PAD] = edge
        drive[n, :, PAD + width :] = edge

    def one_hot(index, height):
        at = lax.broadcasted_iota(jnp.int32, (height, index.shape[1]), 0)
        return jnp.where(at == index, 1.0, 0.0)

    first_row = me * (depth * width)
    src = src_cells[...]
    src_row = lax.div(src, lanes)
    src_lane = src - src_row * lanes
    src_at = (one_hot(src_lane, lanes) * src_signs[...].astype(jnp.float32)).astype(jnp.bfloat16)
    src_rows = one_hot(src_row - first_row, depth * width).astype(jnp.bfloat16)
    source[...] = contract_lanes(src_rows, src_at).reshape(depth, width, lanes)

    def place_receivers():
        rec = rec_cells[...]
        rec_row = lax.div(rec, lanes)
        rec_lane = rec - rec_row * lanes
        at_lane = one_hot(rec_lane, lanes)
        pieces[0:lanes] = at_lane.astype(jnp.bfloat16)
        for n in range(STEPS):
            rest = at_lane * observed[0, n : n + 1, :]
            for k in range(3):
                part = rest.astype(jnp.bfloat16)
                begin = (1 + 3 * n + k) * lanes
                pieces[begin : begin + lanes] = part
                rest = rest - part.astype(jnp.float32)
        hot_rows[...] = one_hot(rec_row - first_row, depth * width).astype(jnp.bfloat16)
        count[...] = contract_lanes(hot_rows[...], pieces[0:lanes]).reshape(depth, width, lanes)

    def place_observed(n):
        begin = (1 + 3 * n) * lanes
        got = contract_lanes(hot_rows[...], pieces[begin : begin + 3 * lanes])
        got = (got[:, 2 * lanes :] + got[:, lanes : 2 * lanes]) + got[:, :lanes]
        seen[n] = got.reshape(depth, width, lanes)

    loads[1].wait()
    for d in range(depth):
        s = slow[d]
        held = courant / (s * s)
        scaled[d] = held
        factor[d] = (-2.0 * held) / s
    for k in (0, 2, 3, 4, 5):
        loads[k].wait()

    lane = lax.broadcasted_iota(jnp.int32, (8, lanes), 1)[:1]
    left_1 = jnp.where(lane >= 1, near_coef, 0.0)
    left_2 = jnp.where(lane >= 2, far_coef, 0.0)
    right_1 = jnp.where(lane < lanes - 1, near_coef, 0.0)
    right_2 = jnp.where(lane < lanes - 2, far_coef, 0.0)

    def laplace(ref, n, stage, r):
        def rows_at(d, shift):
            return ref[n, d, pl.ds(r + PAD + shift, SUB)]

        low = [halo[stage, 0, k, pl.ds(r, SUB)] for k in range(LINK)]
        mids = [rows_at(d, 0) for d in range(depth)]
        high = [halo[stage, 1, k, pl.ds(r, SUB)] for k in range(LINK)]
        planes = low + mids + high
        curved = []
        for d in range(depth):
            mid = mids[d]
            near = (planes[d + 1] + planes[d + 3]) + (rows_at(d, -1) + rows_at(d, 1))
            far = (planes[d] + planes[d + 4]) + (rows_at(d, -2) + rows_at(d, 2))
            along = (
                left_1 * pltpu.roll(mid, 1, 1)
                + right_1 * pltpu.roll(mid, lanes - 1, 1)
                + left_2 * pltpu.roll(mid, 2, 1)
                + right_2 * pltpu.roll(mid, lanes - 2, 1)
            )
            curved.append(
                (3.0 * center_coef) * mid + near_coef * near + far_coef * far + along
            )
        return curved, mids

    def blocks(c, body):
        for k in range(rows // SUB):
            body(pl.multiple_of(c * rows + k * SUB, 8))

    def adjoint_part(level, d, r, back, begin_accum):
        at = pl.ds(r, SUB)
        up = back + (
            count[d, at] * field[level + 1, d, pl.ds(r + PAD, SUB)] - seen[level, d, at]
        )
        term = up * saved[level, d, at]
        term = term if begin_accum else accum[d, at] + term
        if level == 0:
            grad[d, at] = term * factor[d, at]
            return
        accum[d, at] = term
        united[level, d, at] = up
        pushed = scaled[d, at] * up
        out = pushed
        for m in range(MECH):
            if begin_accum:
                back_relax[m, d, at] = pushed
            else:
                held = back_relax[m, d, at]
                out = out - relax_weight[m] * held
                if level > 1:
                    back_relax[m, d, at] = relax_decay[m] * held + pushed
        drive[STEPS - 1 - level, d, pl.ds(r + PAD, SUB)] = out

    def forward_stage(n):
        amount = wavelet[n]

        def chunk(c, carry):
            wait_halo(n, c)
            if n > 0:
                wait_sent(n - 1, c)

            def body(r):
                at = pl.ds(r, SUB)
                inner = pl.ds(r + PAD, SUB)
                curved, mids = laplace(field, n, n, r)
                for d in range(depth):
                    held = [relax[m, d, at] for m in range(MECH)]
                    accel = curved[d] + ((held[0] + held[1]) + held[2])
                    before = older[d, at] if n == 0 else field[n - 1, d, inner]
                    newer = (2.0 * mids[d] - before) + scaled[d, at] * accel
                    newer = newer + amount * source[d, at]
                    saved[n, d, at] = accel
                    field[n + 1, d, inner] = newer
                    if n < STEPS - 1:
                        for m in range(MECH):
                            relax[m, d, at] = (
                                relax_decay[m] * held[m] - relax_weight[m] * curved[d]
                            )
                    else:
                        adjoint_part(n, d, r, adj_now[d, at], True)

            blocks(c, body)
            send_halo(n + 1, c)
            return carry

        lax.fori_loop(0, CHUNKS, chunk, 0)

    piece = depth * rows // shots

    def spot(owner, c):
        begin = owner * piece
        return begin // rows, pl.multiple_of(c * rows + begin % rows, 8)

    def part_copy(k, c):
        target = lax.rem(shot + k, shots)
        d, r = spot(target, c)
        return pltpu.make_async_remote_copy(
            src_ref=grad.at[d, pl.ds(r, piece)],
            dst_ref=parts.at[c, k - 1],
            send_sem=part_send.at[c, k - 1],
            recv_sem=part_recv.at[c, k - 1],
            device_id={"shot": target},
            device_id_type=MESH,
        )

    def whole_copy(k, c):
        target = lax.rem(shot + k, shots)
        d, r = spot(shot, c)
        return pltpu.make_async_remote_copy(
            src_ref=total.at[d, pl.ds(r, piece)],
            dst_ref=total.at[d, pl.ds(r, piece)],
            send_sem=whole_send.at[c, k - 1],
            recv_sem=whole_recv.at[c, k - 1],
            device_id={"shot": target},
            device_id_type=MESH,
        )

    def reduce_chunk(c):
        d, r = spot(shot, c)
        held = grad[d, pl.ds(r, piece)]
        for k in range(1, shots):
            part_copy(k, c).wait_recv()
            held = held + parts[c, k - 1]
        total[d, pl.ds(r, piece)] = held
        for k in range(1, shots):
            whole_copy(k, c).start()

    def backward_stage(level):
        stage = 2 * STEPS - 2 - level

        def chunk(c, carry):
            wait_halo(stage, c)
            wait_sent(stage - 1, c)

            def body(r):
                at = pl.ds(r, SUB)
                curved, _ = laplace(drive, stage - STEPS, stage, r)
                for d in range(depth):
                    after = united[level + 1, d, at]
                    if level == STEPS - 2:
                        base = adj_prev[d, at]
                    else:
                        base = -united[level + 2, d, at]
                    adjoint_part(level, d, r, (base + 2.0 * after) + curved[d], False)

            blocks(c, body)
            if level > 0:
                send_halo(stage + 1, c)
            else:
                for k in range(1, shots):
                    part_copy(k, c).start()

                @pl.when(c >= 2)
                def _():
                    reduce_chunk(c - 2)

            return carry

        lax.fori_loop(0, CHUNKS, chunk, 0)

    for n in range(STEPS):
        forward_stage(n)
        if n == 0:
            place_receivers()
        if n in (1, 2):
            for k in (2 * n - 2, 2 * n - 1):
                place_observed(k)
    for level in reversed(range(STEPS - 1)):
        backward_stage(level)
    for c in range(CHUNKS - 2, CHUNKS):
        reduce_chunk(c)

    def settle(c, carry):
        wait_sent(stages - 1, c)
        for k in range(1, shots):
            part_copy(k, c).wait_send()
            whole_copy(k, c).wait()
        return carry

    lax.fori_loop(0, CHUNKS, settle, 0)

    store = pltpu.make_async_copy(total, total_out, load_sem.at[0])
    store.start()

    summed = jnp.zeros((8, lanes), jnp.float32)
    for d in range(depth):
        block = total[d]
        summed = summed + jnp.sum((block * block).reshape(width // 8, 8, lanes), axis=0)
    squares[me] = summed

    def square_copy(k):
        return pltpu.make_async_remote_copy(
            src_ref=squares.at[me],
            dst_ref=squares.at[me],
            send_sem=square_send.at[k - 1],
            recv_sem=square_recv.at[k - 1],
            device_id={"slab": lax.rem(me + k, slabs)},
            device_id_type=MESH,
        )

    for k in range(1, slabs):
        square_copy(k).start()
    for k in range(1, slabs):
        square_copy(k).wait()
    everything = squares[0]
    for k in range(1, slabs):
        everything = everything + squares[k]
    cells = slabs * depth * width * lanes
    mean = jnp.sum(everything, keepdims=True) / cells + tiny_eps
    inv_out[...] = jnp.broadcast_to(1.0 / jnp.sqrt(mean), inv_out.shape)
    store.wait()


def finish(total, slowness, inverse, new_slowness, gradient):
    share = gradient.shape[1]
    first = pl.multiple_of(lax.axis_index("shot") * share, 8)
    inv = inverse[0:1]
    for d in range(total.shape[0]):
        new_slowness[d] = slowness[d] - update_rate * (total[d] * inv)
        gradient[d] = total[d, pl.ds(first, share)] * inv


def per_device(
    slowness,
    wave_prev,
    wave_now,
    memory,
    adjoint_now,
    adjoint_prev,
    wavelet,
    src_cells,
    src_signs,
    rec_cells,
    observed,
):
    depth, width, lanes = slowness.shape
    shots, slabs = lax.axis_size("shot"), lax.axis_size("slab")
    rows = width // CHUNKS
    piece = depth * rows // shots
    assert width % CHUNKS == 0 and rows % SUB == 0 and depth >= LINK
    assert depth * rows % shots == 0 and rows % piece == 0 and piece % 8 == 0
    receivers = rec_cells.shape[0]
    stages = 2 * STEPS - 1
    f32 = jnp.float32
    block = (depth, width, lanes)
    padded = (depth, width + 2 * PAD, lanes)
    anywhere = pl.BlockSpec(memory_space=pl.ANY)
    vmem = pl.BlockSpec(memory_space=pltpu.VMEM)
    smem = pl.BlockSpec(memory_space=pltpu.SMEM)
    dma = pltpu.SemaphoreType.DMA
    total, inverse = pl.pallas_call(
        functools.partial(kernel, shots, slabs),
        name="invert",
        out_shape=(
            jax.ShapeDtypeStruct(block, f32),
            jax.ShapeDtypeStruct((8, lanes), f32),
        ),
        in_specs=[anywhere] * 6 + [smem] + [vmem] * 4,
        out_specs=(anywhere, vmem),
        scratch_shapes=[
            pltpu.VMEM(block, f32),
            pltpu.VMEM(block, f32),
            pltpu.VMEM((STEPS + 1, *padded), f32),
            pltpu.VMEM((MECH, *block), f32),
            pltpu.VMEM(block, f32),
            pltpu.VMEM(block, f32),
            pltpu.VMEM((STEPS - 1, *padded), f32),
            pltpu.VMEM((STEPS, *block), f32),
            pltpu.VMEM((STEPS, *block), f32),
            pltpu.VMEM((MECH, *block), f32),
            pltpu.VMEM(block, f32),
            pltpu.VMEM(block, f32),
            pltpu.VMEM(block, f32),
            pltpu.VMEM(block, f32),
            pltpu.VMEM((STEPS, *block), f32),
            pltpu.VMEM(block, f32),
            pltpu.VMEM((depth * width, receivers), jnp.bfloat16),
            pltpu.VMEM(((1 + 3 * STEPS) * lanes, receivers), jnp.bfloat16),
            pltpu.VMEM((stages, 2, LINK, width, lanes), f32),
            pltpu.VMEM(block, f32),
            pltpu.VMEM((CHUNKS, shots - 1, piece, lanes), f32),
            pltpu.VMEM(block, f32),
            pltpu.VMEM((slabs, 8, lanes), f32),
            dma((6,)),
            dma((stages, 2, CHUNKS)),
            dma((stages, 2, CHUNKS)),
            dma((CHUNKS, shots - 1)),
            dma((CHUNKS, shots - 1)),
            dma((CHUNKS, shots - 1)),
            dma((CHUNKS, shots - 1)),
            dma((slabs - 1,)),
            dma((slabs - 1,)),
        ],
        compiler_params=pltpu.CompilerParams(
            collective_id=0, has_side_effects=True, vmem_limit_bytes=60 * 2**20
        ),
    )(
        slowness,
        wave_prev,
        wave_now,
        memory,
        adjoint_now,
        adjoint_prev,
        wavelet,
        src_cells,
        src_signs,
        rec_cells.reshape(1, receivers),
        observed,
    )
    share = width // shots
    new_slowness, gradient = pl.pallas_call(
        finish,
        name="finish",
        out_shape=(
            jax.ShapeDtypeStruct(block, f32),
            jax.ShapeDtypeStruct((depth, share, lanes), f32),
        ),
        in_specs=[vmem] * 3,
        out_specs=(vmem, vmem),
        compiler_params=pltpu.CompilerParams(vmem_limit_bytes=60 * 2**20),
    )(total, slowness, inverse)
    return (new_slowness, gradient)


def solution(mesh):
    in_specs = (
        P(("groups", "slab"), None, None),
        P(("groups", "shot"), "slab", None, None),
        P(("groups", "shot"), "slab", None, None),
        P(("groups", "shot"), None, "slab", None, None),
        P(("groups", "shot"), "slab", None, None),
        P(("groups", "shot"), "slab", None, None),
        P(),
        P(("groups", "shot"), None),
        P(("groups", "shot"), None),
        P("groups"),
        P(("groups", "shot"), None, None),
    )
    out_specs = (P(("groups", "slab"), None, None), P(("groups", "slab"), "shot", None))
    return jax.shard_map(
        per_device, mesh=mesh, in_specs=in_specs, out_specs=out_specs, check_vma=False
    )
```

```python
import functools

import jax
import jax.numpy as jnp
from jax import lax
from jax.experimental import pallas as pl
from jax.experimental.pallas import tpu as pltpu
from jax.sharding import PartitionSpec as P

STEPS = 4
MECH = 3
LINK = 2
PAD = 8
CHUNKS = 4
SUB = 24

center_coef = -2.5
near_coef = 4.0 / 3.0
far_coef = -1.0 / 12.0
courant = 0.14
relax_decay = (0.3, 0.7, 0.95)
relax_weight = (0.3, 0.2, 0.1)
update_rate = 0.05
tiny_eps = 1e-06

lag_weight = tuple(
    sum(w * a**j for w, a in zip(relax_weight, relax_decay)) for j in range(STEPS - 1)
)

MESH = pl.DeviceIdType.MESH


def contract_lanes(a, b):
    return lax.dot_general(a, b, (((1,), (1,)), ((), ())), preferred_element_type=jnp.float32)


def kernel(
    shots,
    slabs,
    slowness_in,
    prev_in,
    now_in,
    memory_in,
    adj_now_in,
    adj_prev_in,
    wavelet,
    src_cells,
    src_signs,
    rec_cells,
    observed,
    total_out,
    inv_out,
    slow,
    older,
    field,
    relax,
    adj_now,
    adj_prev,
    drive,
    united,
    saved,
    fading,
    curves,
    pushes,
    accum,
    scaled,
    factor,
    count,
    seen,
    source,
    hot_rows,
    pieces,
    halo,
    grad,
    parts,
    total,
    squares,
    sums,
    load_sem,
    halo_send,
    halo_recv,
    part_send,
    part_recv,
    whole_send,
    whole_recv,
    square_send,
    square_recv,
    sum_send,
    sum_recv,
):
    depth, width, lanes = slow.shape
    rows = width // CHUNKS
    stages = 2 * STEPS - 1
    me = lax.axis_index("slab")
    shot = lax.axis_index("shot")

    loads = [
        pltpu.make_async_copy(now_in.at[0], field.at[0, :, PAD : PAD + width], load_sem.at[0]),
        pltpu.make_async_copy(slowness_in, slow, load_sem.at[1]),
        pltpu.make_async_copy(memory_in.at[0], relax, load_sem.at[2]),
        pltpu.make_async_copy(prev_in.at[0], older, load_sem.at[3]),
        pltpu.make_async_copy(adj_now_in.at[0], adj_now, load_sem.at[4]),
        pltpu.make_async_copy(adj_prev_in.at[0], adj_prev, load_sem.at[5]),
    ]
    barrier = pltpu.get_barrier_semaphore()
    for k in range(1, slabs):
        pl.semaphore_signal(
            barrier, inc=1, device_id={"slab": lax.rem(me + k, slabs)}, device_id_type=MESH
        )
    for k in range(1, shots):
        pl.semaphore_signal(
            barrier, inc=1, device_id={"shot": lax.rem(shot + k, shots)}, device_id_type=MESH
        )
    for copy in loads:
        copy.start()
    pl.semaphore_wait(barrier, slabs - 1 + shots - 1)

    def outgoing(stage, side, c):
        first = depth - LINK if side == 0 else 0
        planes = pl.ds(first, LINK)
        start = pl.multiple_of(c * rows, 8)
        if stage == 0:
            src = now_in.at[0, planes, pl.ds(start, rows)]
        elif stage < STEPS:
            src = field.at[stage, planes, pl.ds(start + PAD, rows)]
        else:
            src = drive.at[stage - STEPS, planes, pl.ds(start + PAD, rows)]
        target = me + 1 if side == 0 else me - 1
        return pltpu.make_async_remote_copy(
            src_ref=src,
            dst_ref=halo.at[stage, side, :, pl.ds(start, rows)],
            send_sem=halo_send.at[stage, side, c],
            recv_sem=halo_recv.at[stage, side, c],
            device_id={"slab": target},
            device_id_type=MESH,
        )

    has_up = me < slabs - 1
    has_down = me > 0

    def send_halo(stage, c):
        @pl.when(has_up)
        def _():
            outgoing(stage, 0, c).start()

        @pl.when(has_down)
        def _():
            outgoing(stage, 1, c).start()

    def wait_sent(stage, c):
        @pl.when(has_up)
        def _():
            outgoing(stage, 0, c).wait_send()

        @pl.when(has_down)
        def _():
            outgoing(stage, 1, c).wait_send()

    def wait_halo(stage, c):
        @pl.when(has_down)
        def _():
            outgoing(stage, 0, c).wait_recv()

        @pl.when(has_up)
        def _():
            outgoing(stage, 1, c).wait_recv()

    for c in range(CHUNKS):
        send_halo(0, c)

    @pl.when(jnp.logical_not(has_down))
    def _():
        halo[:, 0] = jnp.zeros((stages, LINK, width, lanes), jnp.float32)

    @pl.when(jnp.logical_not(has_up))
    def _():
        halo[:, 1] = jnp.zeros((stages, LINK, width, lanes), jnp.float32)

    edge = jnp.zeros((depth, PAD, lanes), jnp.float32)
    for n in range(STEPS):
        field[n, :, :PAD] = edge
        field[n, :, PAD + width :] = edge
    for n in range(STEPS - 1):
        drive[n, :, :PAD] = edge
        drive[n, :, PAD + width :] = edge

    def one_hot(index, height):
        at = lax.broadcasted_iota(jnp.int32, (height, index.shape[1]), 0)
        return jnp.where(at == index, 1.0, 0.0)

    first_row = me * (depth * width)
    src = src_cells[...]
    src_row = lax.div(src, lanes)
    src_lane = src - src_row * lanes
    src_at = (one_hot(src_lane, lanes) * src_signs[...].astype(jnp.float32)).astype(jnp.bfloat16)
    src_rows = one_hot(src_row - first_row, depth * width).astype(jnp.bfloat16)
    source[...] = contract_lanes(src_rows, src_at).reshape(depth, width, lanes)

    def place_receivers():
        rec = rec_cells[...]
        rec_row = lax.div(rec, lanes)
        rec_lane = rec - rec_row * lanes
        at_lane = one_hot(rec_lane, lanes)
        pieces[0:lanes] = at_lane.astype(jnp.bfloat16)
        for n in range(STEPS):
            rest = at_lane * observed[0, n : n + 1, :]
            for k in range(3):
                part = rest.astype(jnp.bfloat16)
                begin = (1 + 3 * n + k) * lanes
                pieces[begin : begin + lanes] = part
                rest = rest - part.astype(jnp.float32)
        hot_rows[...] = one_hot(rec_row - first_row, depth * width).astype(jnp.bfloat16)
        count[...] = contract_lanes(hot_rows[...], pieces[0:lanes]).reshape(depth, width, lanes)

    def place_observed(n):
        begin = (1 + 3 * n) * lanes
        got = contract_lanes(hot_rows[...], pieces[begin : begin + 3 * lanes])
        got = (got[:, 2 * lanes :] + got[:, lanes : 2 * lanes]) + got[:, :lanes]
        seen[n] = got.reshape(depth, width, lanes)

    loads[1].wait()
    for d in range(depth):
        s = slow[d]
        held = courant / (s * s)
        scaled[d] = held
        factor[d] = (-2.0 * held) / s
    loads[2].wait()

    def fade(k, carry):
        at = pl.ds(pl.multiple_of(k * SUB, 8), SUB)
        for d in range(depth):
            held = [relax[m, d, at] for m in range(MECH)]
            for n in range(STEPS):
                fading[n, d, at] = (held[0] + held[1]) + held[2]
                held = [relax_decay[m] * held[m] for m in range(MECH)]
        return carry

    lax.fori_loop(0, width // SUB, fade, 0)
    for k in (0, 3, 4, 5):
        loads[k].wait()

    lane = lax.broadcasted_iota(jnp.int32, (8, lanes), 1)[:1]
    left_1 = jnp.where(lane >= 1, near_coef, 0.0)
    left_2 = jnp.where(lane >= 2, far_coef, 0.0)
    right_1 = jnp.where(lane < lanes - 1, near_coef, 0.0)
    right_2 = jnp.where(lane < lanes - 2, far_coef, 0.0)

    def laplace(ref, n, stage, r):
        def rows_at(d, shift):
            return ref[n, d, pl.ds(r + PAD + shift, SUB)]

        low = [halo[stage, 0, k, pl.ds(r, SUB)] for k in range(LINK)]
        mids = [rows_at(d, 0) for d in range(depth)]
        high = [halo[stage, 1, k, pl.ds(r, SUB)] for k in range(LINK)]
        planes = low + mids + high
        curved = []
        for d in range(depth):
            mid = mids[d]
            near = (planes[d + 1] + planes[d + 3]) + (rows_at(d, -1) + rows_at(d, 1))
            far = (planes[d] + planes[d + 4]) + (rows_at(d, -2) + rows_at(d, 2))
            along = (
                left_1 * pltpu.roll(mid, 1, 1)
                + right_1 * pltpu.roll(mid, lanes - 1, 1)
                + left_2 * pltpu.roll(mid, 2, 1)
                + right_2 * pltpu.roll(mid, lanes - 2, 1)
            )
            curved.append(
                (3.0 * center_coef) * mid + near_coef * near + far_coef * far + along
            )
        return curved, mids

    def blocks(c, body):
        for k in range(rows // SUB):
            body(pl.multiple_of(c * rows + k * SUB, 8))

    def adjoint_part(level, d, r, back, begin_accum):
        at = pl.ds(r, SUB)
        up = back + (
            count[d, at] * field[level + 1, d, pl.ds(r + PAD, SUB)] - seen[level, d, at]
        )
        term = up * saved[level, d, at]
        term = term if begin_accum else accum[d, at] + term
        if level == 0:
            grad[d, at] = term * factor[d, at]
            return
        accum[d, at] = term
        united[level, d, at] = up
        pushed = scaled[d, at] * up
        out = pushed
        if level == STEPS - 2:
            pushes[d, at] = pushed
            out = pushed - lag_weight[0] * drive[0, d, pl.ds(r + PAD, SUB)]
        elif level == STEPS - 3:
            out = (pushed - lag_weight[0] * pushes[d, at]) - lag_weight[1] * drive[
                0, d, pl.ds(r + PAD, SUB)
            ]
        drive[STEPS - 1 - level, d, pl.ds(r + PAD, SUB)] = out

    def forward_stage(n):
        amount = wavelet[n]

        def chunk(c, carry):
            wait_halo(n, c)
            if n > 0:
                wait_sent(n - 1, c)

            def body(r):
                at = pl.ds(r, SUB)
                inner = pl.ds(r + PAD, SUB)
                curved, mids = laplace(field, n, n, r)
                for d in range(depth):
                    accel = curved[d] + fading[n, d, at]
                    for m in range(n):
                        accel = accel - lag_weight[n - 1 - m] * curves[m, d, at]
                    before = older[d, at] if n == 0 else field[n - 1, d, inner]
                    newer = (2.0 * mids[d] - before) + scaled[d, at] * accel
                    newer = newer + amount * source[d, at]
                    saved[n, d, at] = accel
                    field[n + 1, d, inner] = newer
                    if n < STEPS - 1:
                        curves[n, d, at] = curved[d]
                    else:
                        adjoint_part(n, d, r, adj_now[d, at], True)

            blocks(c, body)
            send_halo(n + 1, c)
            return carry

        lax.fori_loop(0, CHUNKS, chunk, 0)

    piece = depth * rows // shots

    def spot(owner, c):
        begin = owner * piece
        return begin // rows, pl.multiple_of(c * rows + begin % rows, 8)

    def part_copy(k, c):
        target = lax.rem(shot + k, shots)
        d, r = spot(target, c)
        return pltpu.make_async_remote_copy(
            src_ref=grad.at[d, pl.ds(r, piece)],
            dst_ref=parts.at[c, k - 1],
            send_sem=part_send.at[c, k - 1],
            recv_sem=part_recv.at[c, k - 1],
            device_id={"shot": target},
            device_id_type=MESH,
        )

    def whole_copy(k, c):
        target = lax.rem(shot + k, shots)
        d, r = spot(shot, c)
        return pltpu.make_async_remote_copy(
            src_ref=total.at[d, pl.ds(r, piece)],
            dst_ref=total.at[d, pl.ds(r, piece)],
            send_sem=whole_send.at[c, k - 1],
            recv_sem=whole_recv.at[c, k - 1],
            device_id={"shot": target},
            device_id_type=MESH,
        )

    def reduce_chunk(c):
        d, r = spot(shot, c)
        held = grad[d, pl.ds(r, piece)]
        for k in range(1, shots):
            part_copy(k, c).wait_recv()
            held = held + parts[c, k - 1]
        total[d, pl.ds(r, piece)] = held
        for k in range(1, shots):
            whole_copy(k, c).start()

    def backward_stage(level):
        stage = 2 * STEPS - 2 - level

        def chunk(c, carry):
            wait_halo(stage, c)
            wait_sent(stage - 1, c)

            def body(r):
                at = pl.ds(r, SUB)
                curved, _ = laplace(drive, stage - STEPS, stage, r)
                for d in range(depth):
                    after = united[level + 1, d, at]
                    if level == STEPS - 2:
                        base = adj_prev[d, at]
                    else:
                        base = -united[level + 2, d, at]
                    adjoint_part(level, d, r, (base + 2.0 * after) + curved[d], False)

            blocks(c, body)
            if level > 0:
                send_halo(stage + 1, c)
            else:
                for k in range(1, shots):
                    part_copy(k, c).start()

                @pl.when(c >= 2)
                def _():
                    reduce_chunk(c - 2)

            return carry

        lax.fori_loop(0, CHUNKS, chunk, 0)

    for n in range(STEPS):
        forward_stage(n)
        if n == 0:
            place_receivers()
        if n in (1, 2):
            for k in (2 * n - 2, 2 * n - 1):
                place_observed(k)
    for level in reversed(range(STEPS - 1)):
        backward_stage(level)
    for c in range(CHUNKS - 2, CHUNKS):
        reduce_chunk(c)

    summed = jnp.zeros((8, lanes), jnp.float32)
    for c in range(CHUNKS):
        d, r = spot(shot, c)
        held = total[d, pl.ds(r, piece)]
        summed = summed + jnp.sum((held * held).reshape(piece // 8, 8, lanes), axis=0)
    squares[me] = summed

    def square_copy(k):
        return pltpu.make_async_remote_copy(
            src_ref=squares.at[me],
            dst_ref=squares.at[me],
            send_sem=square_send.at[k - 1],
            recv_sem=square_recv.at[k - 1],
            device_id={"slab": lax.rem(me + k, slabs)},
            device_id_type=MESH,
        )

    def shot_copy(k):
        return pltpu.make_async_remote_copy(
            src_ref=sums.at[shot],
            dst_ref=sums.at[shot],
            send_sem=sum_send.at[k - 1],
            recv_sem=sum_recv.at[k - 1],
            device_id={"shot": lax.rem(shot + k, shots)},
            device_id_type=MESH,
        )

    for k in range(1, slabs):
        square_copy(k).start()

    def settle_parts(c, carry):
        wait_sent(stages - 1, c)
        for k in range(1, shots):
            part_copy(k, c).wait_send()
        return carry

    lax.fori_loop(0, CHUNKS, settle_parts, 0)
    for k in range(1, slabs):
        square_copy(k).wait_recv()
    everything = squares[0]
    for k in range(1, slabs):
        everything = everything + squares[k]
    sums[shot] = everything
    for k in range(1, shots):
        shot_copy(k).start()

    def settle(c, carry):
        for k in range(1, shots):
            whole_copy(k, c).wait()
        return carry

    lax.fori_loop(0, CHUNKS, settle, 0)
    store = pltpu.make_async_copy(total, total_out, load_sem.at[0])
    store.start()
    for k in range(1, slabs):
        square_copy(k).wait_send()
    for k in range(1, shots):
        shot_copy(k).wait()
    everything = sums[0]
    for k in range(1, shots):
        everything = everything + sums[k]
    cells = slabs * depth * width * lanes
    mean = jnp.sum(everything, keepdims=True) / cells + tiny_eps
    inv_out[...] = jnp.broadcast_to(1.0 / jnp.sqrt(mean), inv_out.shape)
    store.wait()


def finish(total, slowness, inverse, new_slowness, gradient):
    share = gradient.shape[1]
    first = pl.multiple_of(lax.axis_index("shot") * share, 8)
    inv = inverse[0:1]
    for d in range(total.shape[0]):
        new_slowness[d] = slowness[d] - update_rate * (total[d] * inv)
        gradient[d] = total[d, pl.ds(first, share)] * inv


def per_device(
    slowness,
    wave_prev,
    wave_now,
    memory,
    adjoint_now,
    adjoint_prev,
    wavelet,
    src_cells,
    src_signs,
    rec_cells,
    observed,
):
    depth, width, lanes = slowness.shape
    shots, slabs = lax.axis_size("shot"), lax.axis_size("slab")
    rows = width // CHUNKS
    piece = depth * rows // shots
    assert width % CHUNKS == 0 and rows % SUB == 0 and depth >= LINK
    assert depth * rows % shots == 0 and rows % piece == 0 and piece % 8 == 0
    receivers = rec_cells.shape[0]
    stages = 2 * STEPS - 1
    f32 = jnp.float32
    block = (depth, width, lanes)
    padded = (depth, width + 2 * PAD, lanes)
    anywhere = pl.BlockSpec(memory_space=pl.ANY)
    vmem = pl.BlockSpec(memory_space=pltpu.VMEM)
    smem = pl.BlockSpec(memory_space=pltpu.SMEM)
    dma = pltpu.SemaphoreType.DMA
    total, inverse = pl.pallas_call(
        functools.partial(kernel, shots, slabs),
        name="invert",
        out_shape=(
            jax.ShapeDtypeStruct(block, f32),
            jax.ShapeDtypeStruct((8, lanes), f32),
        ),
        in_specs=[anywhere] * 6 + [smem] + [vmem] * 4,
        out_specs=(anywhere, vmem),
        scratch_shapes=[
            pltpu.VMEM(block, f32),
            pltpu.VMEM(block, f32),
            pltpu.VMEM((STEPS + 1, *padded), f32),
            pltpu.VMEM((MECH, *block), f32),
            pltpu.VMEM(block, f32),
            pltpu.VMEM(block, f32),
            pltpu.VMEM((STEPS - 1, *padded), f32),
            pltpu.VMEM((STEPS, *block), f32),
            pltpu.VMEM((STEPS, *block), f32),
            pltpu.VMEM((STEPS, *block), f32),
            pltpu.VMEM((STEPS - 1, *block), f32),
            pltpu.VMEM(block, f32),
            pltpu.VMEM(block, f32),
            pltpu.VMEM(block, f32),
            pltpu.VMEM(block, f32),
            pltpu.VMEM(block, f32),
            pltpu.VMEM((STEPS, *block), f32),
            pltpu.VMEM(block, f32),
            pltpu.VMEM((depth * width, receivers), jnp.bfloat16),
            pltpu.VMEM(((1 + 3 * STEPS) * lanes, receivers), jnp.bfloat16),
            pltpu.VMEM((stages, 2, LINK, width, lanes), f32),
            pltpu.VMEM(block, f32),
            pltpu.VMEM((CHUNKS, shots - 1, piece, lanes), f32),
            pltpu.VMEM(block, f32),
            pltpu.VMEM((slabs, 8, lanes), f32),
            pltpu.VMEM((shots, 8, lanes), f32),
            dma((6,)),
            dma((stages, 2, CHUNKS)),
            dma((stages, 2, CHUNKS)),
            dma((CHUNKS, shots - 1)),
            dma((CHUNKS, shots - 1)),
            dma((CHUNKS, shots - 1)),
            dma((CHUNKS, shots - 1)),
            dma((slabs - 1,)),
            dma((slabs - 1,)),
            dma((shots - 1,)),
            dma((shots - 1,)),
        ],
        compiler_params=pltpu.CompilerParams(
            collective_id=0, has_side_effects=True, vmem_limit_bytes=60 * 2**20
        ),
    )(
        slowness,
        wave_prev,
        wave_now,
        memory,
        adjoint_now,
        adjoint_prev,
        wavelet,
        src_cells,
        src_signs,
        rec_cells.reshape(1, receivers),
        observed,
    )
    share = width // shots
    new_slowness, gradient = pl.pallas_call(
        finish,
        name="finish",
        out_shape=(
            jax.ShapeDtypeStruct(block, f32),
            jax.ShapeDtypeStruct((depth, share, lanes), f32),
        ),
        in_specs=[vmem] * 3,
        out_specs=(vmem, vmem),
        compiler_params=pltpu.CompilerParams(vmem_limit_bytes=60 * 2**20),
    )(total, slowness, inverse)
    return (new_slowness, gradient)


def solution(mesh):
    in_specs = (
        P(("groups", "slab"), None, None),
        P(("groups", "shot"), "slab", None, None),
        P(("groups", "shot"), "slab", None, None),
        P(("groups", "shot"), None, "slab", None, None),
        P(("groups", "shot"), "slab", None, None),
        P(("groups", "shot"), "slab", None, None),
        P(),
        P(("groups", "shot"), None),
        P(("groups", "shot"), None),
        P("groups"),
        P(("groups", "shot"), None, None),
    )
    out_specs = (P(("groups", "slab"), None, None), P(("groups", "slab"), "shot", None))
    return jax.shard_map(
        per_device, mesh=mesh, in_specs=in_specs, out_specs=out_specs, check_vma=False
    )
```

```python
import functools

import jax
import jax.numpy as jnp
from jax import lax
from jax.experimental import pallas as pl
from jax.experimental.pallas import tpu as pltpu
from jax.sharding import PartitionSpec as P

STEPS = 4
MECH = 3
LINK = 2
PAD = 8
CHUNKS = 3
SUB = 32

center_coef = -2.5
near_coef = 4.0 / 3.0
far_coef = -1.0 / 12.0
courant = 0.14
relax_decay = (0.3, 0.7, 0.95)
relax_weight = (0.3, 0.2, 0.1)
update_rate = 0.05
tiny_eps = 1e-06

lag_weight = tuple(
    sum(w * a**j for w, a in zip(relax_weight, relax_decay)) for j in range(STEPS - 1)
)

MESH = pl.DeviceIdType.MESH


def contract_lanes(a, b):
    return lax.dot_general(a, b, (((1,), (1,)), ((), ())), preferred_element_type=jnp.float32)


def kernel(
    shots,
    slabs,
    slowness_in,
    prev_in,
    now_in,
    memory_in,
    adj_now_in,
    adj_prev_in,
    wavelet_in,
    src_cells_in,
    src_signs_in,
    rec_cells_in,
    observed_in,
    total_out,
    inv_out,
    slow,
    older,
    field,
    relax,
    adj_now,
    adj_prev,
    drive,
    united,
    saved,
    fading,
    curves,
    pushes,
    accum,
    scaled,
    factor,
    count,
    seen,
    source,
    hot_rows,
    pieces,
    halo,
    grad,
    parts,
    total,
    squares,
    sums,
    wavelet,
    src_cells,
    src_signs,
    rec_cells,
    observed,
    load_sem,
    halo_send,
    halo_recv,
    part_send,
    part_recv,
    whole_send,
    whole_recv,
    square_send,
    square_recv,
    sum_send,
    sum_recv,
):
    depth, width, lanes = slow.shape
    rows = width // CHUNKS
    stages = 2 * STEPS - 1
    me = lax.axis_index("slab")
    shot = lax.axis_index("shot")

    loads = [
        pltpu.make_async_copy(now_in.at[0], field.at[0, :, PAD : PAD + width], load_sem.at[0]),
        pltpu.make_async_copy(slowness_in, slow, load_sem.at[1]),
        pltpu.make_async_copy(memory_in.at[0], relax, load_sem.at[2]),
        pltpu.make_async_copy(prev_in.at[0], older, load_sem.at[3]),
        pltpu.make_async_copy(adj_now_in.at[0], adj_now, load_sem.at[4]),
        pltpu.make_async_copy(adj_prev_in.at[0], adj_prev, load_sem.at[5]),
        pltpu.make_async_copy(wavelet_in, wavelet, load_sem.at[6]),
        pltpu.make_async_copy(src_cells_in, src_cells, load_sem.at[7]),
        pltpu.make_async_copy(src_signs_in, src_signs, load_sem.at[8]),
        pltpu.make_async_copy(rec_cells_in, rec_cells, load_sem.at[9]),
        pltpu.make_async_copy(observed_in, observed, load_sem.at[10]),
    ]
    barrier = pltpu.get_barrier_semaphore()
    for k in range(1, slabs):
        pl.semaphore_signal(
            barrier, inc=1, device_id={"slab": lax.rem(me + k, slabs)}, device_id_type=MESH
        )
    for k in range(1, shots):
        pl.semaphore_signal(
            barrier, inc=1, device_id={"shot": lax.rem(shot + k, shots)}, device_id_type=MESH
        )
    for copy in loads:
        copy.start()
    pl.semaphore_wait(barrier, slabs - 1 + shots - 1)

    def outgoing(stage, side, c):
        first = depth - LINK if side == 0 else 0
        planes = pl.ds(first, LINK)
        start = pl.multiple_of(c * rows, 8)
        if stage == 0:
            src = now_in.at[0, planes, pl.ds(start, rows)]
        elif stage < STEPS:
            src = field.at[stage, planes, pl.ds(start + PAD, rows)]
        else:
            src = drive.at[stage - STEPS, planes, pl.ds(start + PAD, rows)]
        target = me + 1 if side == 0 else me - 1
        return pltpu.make_async_remote_copy(
            src_ref=src,
            dst_ref=halo.at[stage, side, :, pl.ds(start, rows)],
            send_sem=halo_send.at[stage, side, c],
            recv_sem=halo_recv.at[stage, side, c],
            device_id={"slab": target},
            device_id_type=MESH,
        )

    has_up = me < slabs - 1
    has_down = me > 0

    def send_halo(stage, c):
        @pl.when(has_up)
        def _():
            outgoing(stage, 0, c).start()

        @pl.when(has_down)
        def _():
            outgoing(stage, 1, c).start()

    def wait_sent(stage, c):
        @pl.when(has_up)
        def _():
            outgoing(stage, 0, c).wait_send()

        @pl.when(has_down)
        def _():
            outgoing(stage, 1, c).wait_send()

    def wait_halo(stage, c):
        @pl.when(has_down)
        def _():
            outgoing(stage, 0, c).wait_recv()

        @pl.when(has_up)
        def _():
            outgoing(stage, 1, c).wait_recv()

    for c in range(CHUNKS):
        send_halo(0, c)

    @pl.when(jnp.logical_not(has_down))
    def _():
        halo[:, 0] = jnp.zeros((stages, LINK, width, lanes), jnp.float32)

    @pl.when(jnp.logical_not(has_up))
    def _():
        halo[:, 1] = jnp.zeros((stages, LINK, width, lanes), jnp.float32)

    edge = jnp.zeros((depth, PAD, lanes), jnp.float32)
    for n in range(STEPS):
        field[n, :, :PAD] = edge
        field[n, :, PAD + width :] = edge
    for n in range(STEPS - 1):
        drive[n, :, :PAD] = edge
        drive[n, :, PAD + width :] = edge

    def one_hot(index, height):
        at = lax.broadcasted_iota(jnp.int32, (height, index.shape[1]), 0)
        return jnp.where(at == index, 1.0, 0.0)

    first_row = me * (depth * width)
    for k in range(6, 11):
        loads[k].wait()
    src = src_cells[...]
    src_row = lax.div(src, lanes)
    src_lane = src - src_row * lanes
    src_at = (one_hot(src_lane, lanes) * src_signs[...].astype(jnp.float32)).astype(jnp.bfloat16)
    src_rows = one_hot(src_row - first_row, depth * width).astype(jnp.bfloat16)
    source[...] = contract_lanes(src_rows, src_at).reshape(depth, width, lanes)

    def place_receivers():
        rec = rec_cells[...]
        rec_row = lax.div(rec, lanes)
        rec_lane = rec - rec_row * lanes
        at_lane = one_hot(rec_lane, lanes)
        pieces[0:lanes] = at_lane.astype(jnp.bfloat16)
        for n in range(STEPS):
            rest = at_lane * observed[0, n : n + 1, :]
            for k in range(3):
                part = rest.astype(jnp.bfloat16)
                begin = (1 + 3 * n + k) * lanes
                pieces[begin : begin + lanes] = part
                rest = rest - part.astype(jnp.float32)
        hot_rows[...] = one_hot(rec_row - first_row, depth * width).astype(jnp.bfloat16)
        count[...] = contract_lanes(hot_rows[...], pieces[0:lanes]).reshape(depth, width, lanes)

    def place_observed(n):
        begin = (1 + 3 * n) * lanes
        got = contract_lanes(hot_rows[...], pieces[begin : begin + 3 * lanes])
        got = (got[:, 2 * lanes :] + got[:, lanes : 2 * lanes]) + got[:, :lanes]
        seen[n] = got.reshape(depth, width, lanes)

    loads[1].wait()
    for d in range(depth):
        s = slow[d]
        held = courant / (s * s)
        scaled[d] = held
        factor[d] = (-2.0 * held) / s
    loads[2].wait()

    def fade(k, carry):
        at = pl.ds(pl.multiple_of(k * SUB, 8), SUB)
        for d in range(depth):
            held = [relax[m, d, at] for m in range(MECH)]
            for n in range(STEPS):
                fading[n, d, at] = (held[0] + held[1]) + held[2]
                held = [relax_decay[m] * held[m] for m in range(MECH)]
        return carry

    lax.fori_loop(0, width // SUB, fade, 0)
    for k in (0, 3, 4, 5):
        loads[k].wait()

    lane = lax.broadcasted_iota(jnp.int32, (8, lanes), 1)[:1]
    left_1 = jnp.where(lane >= 1, near_coef, 0.0)
    left_2 = jnp.where(lane >= 2, far_coef, 0.0)
    right_1 = jnp.where(lane < lanes - 1, near_coef, 0.0)
    right_2 = jnp.where(lane < lanes - 2, far_coef, 0.0)

    def laplace(ref, n, stage, r):
        def rows_at(d, shift):
            return ref[n, d, pl.ds(r + PAD + shift, SUB)]

        low = [halo[stage, 0, k, pl.ds(r, SUB)] for k in range(LINK)]
        mids = [rows_at(d, 0) for d in range(depth)]
        high = [halo[stage, 1, k, pl.ds(r, SUB)] for k in range(LINK)]
        planes = low + mids + high
        curved = []
        for d in range(depth):
            mid = mids[d]
            near = (planes[d + 1] + planes[d + 3]) + (rows_at(d, -1) + rows_at(d, 1))
            far = (planes[d] + planes[d + 4]) + (rows_at(d, -2) + rows_at(d, 2))
            along = (
                left_1 * pltpu.roll(mid, 1, 1)
                + right_1 * pltpu.roll(mid, lanes - 1, 1)
                + left_2 * pltpu.roll(mid, 2, 1)
                + right_2 * pltpu.roll(mid, lanes - 2, 1)
            )
            curved.append(
                (3.0 * center_coef) * mid + near_coef * near + far_coef * far + along
            )
        return curved, mids

    def blocks(c, body):
        for k in range(rows // SUB):
            body(pl.multiple_of(c * rows + k * SUB, 8))

    def adjoint_part(level, d, r, back, begin_accum):
        at = pl.ds(r, SUB)
        up = back + (
            count[d, at] * field[level + 1, d, pl.ds(r + PAD, SUB)] - seen[level, d, at]
        )
        term = up * saved[level, d, at]
        term = term if begin_accum else accum[d, at] + term
        if level == 0:
            grad[d, at] = term * factor[d, at]
            return
        accum[d, at] = term
        united[level, d, at] = up
        pushed = scaled[d, at] * up
        out = pushed
        if level == STEPS - 2:
            pushes[d, at] = pushed
            out = pushed - lag_weight[0] * drive[0, d, pl.ds(r + PAD, SUB)]
        elif level == STEPS - 3:
            out = (pushed - lag_weight[0] * pushes[d, at]) - lag_weight[1] * drive[
                0, d, pl.ds(r + PAD, SUB)
            ]
        drive[STEPS - 1 - level, d, pl.ds(r + PAD, SUB)] = out

    def forward_stage(n):
        amount = wavelet[n]

        def chunk(c, carry):
            wait_halo(n, c)
            if n > 0:
                wait_sent(n - 1, c)

            def body(r):
                at = pl.ds(r, SUB)
                inner = pl.ds(r + PAD, SUB)
                curved, mids = laplace(field, n, n, r)
                for d in range(depth):
                    accel = curved[d] + fading[n, d, at]
                    for m in range(n):
                        accel = accel - lag_weight[n - 1 - m] * curves[m, d, at]
                    before = older[d, at] if n == 0 else field[n - 1, d, inner]
                    newer = (2.0 * mids[d] - before) + scaled[d, at] * accel
                    newer = newer + amount * source[d, at]
                    saved[n, d, at] = accel
                    field[n + 1, d, inner] = newer
                    if n < STEPS - 1:
                        curves[n, d, at] = curved[d]
                    else:
                        adjoint_part(n, d, r, adj_now[d, at], True)

            blocks(c, body)
            send_halo(n + 1, c)
            return carry

        lax.fori_loop(0, CHUNKS, chunk, 0)

    piece = depth * rows // shots

    def spot(owner, c):
        begin = owner * piece
        return begin // rows, pl.multiple_of(c * rows + begin % rows, 8)

    def part_copy(k, c):
        target = lax.rem(shot + k, shots)
        d, r = spot(target, c)
        return pltpu.make_async_remote_copy(
            src_ref=grad.at[d, pl.ds(r, piece)],
            dst_ref=parts.at[c, k - 1],
            send_sem=part_send.at[c, k - 1],
            recv_sem=part_recv.at[c, k - 1],
            device_id={"shot": target},
            device_id_type=MESH,
        )

    def whole_copy(k, c):
        target = lax.rem(shot + k, shots)
        d, r = spot(shot, c)
        return pltpu.make_async_remote_copy(
            src_ref=total.at[d, pl.ds(r, piece)],
            dst_ref=total.at[d, pl.ds(r, piece)],
            send_sem=whole_send.at[c, k - 1],
            recv_sem=whole_recv.at[c, k - 1],
            device_id={"shot": target},
            device_id_type=MESH,
        )

    def reduce_chunk(c):
        d, r = spot(shot, c)
        held = grad[d, pl.ds(r, piece)]
        for k in range(1, shots):
            part_copy(k, c).wait_recv()
            held = held + parts[c, k - 1]
        total[d, pl.ds(r, piece)] = held
        for k in range(1, shots):
            whole_copy(k, c).start()

    def backward_stage(level):
        stage = 2 * STEPS - 2 - level

        def chunk(c, carry):
            wait_halo(stage, c)
            wait_sent(stage - 1, c)

            def body(r):
                at = pl.ds(r, SUB)
                curved, _ = laplace(drive, stage - STEPS, stage, r)
                for d in range(depth):
                    after = united[level + 1, d, at]
                    if level == STEPS - 2:
                        base = adj_prev[d, at]
                    else:
                        base = -united[level + 2, d, at]
                    adjoint_part(level, d, r, (base + 2.0 * after) + curved[d], False)

            blocks(c, body)
            if level > 0:
                send_halo(stage + 1, c)
            else:
                for k in range(1, shots):
                    part_copy(k, c).start()

                @pl.when(c >= 2)
                def _():
                    reduce_chunk(c - 2)

            return carry

        lax.fori_loop(0, CHUNKS, chunk, 0)

    for n in range(STEPS):
        forward_stage(n)
        if n == 0:
            place_receivers()
        if n in (1, 2):
            for k in (2 * n - 2, 2 * n - 1):
                place_observed(k)
    for level in reversed(range(STEPS - 1)):
        backward_stage(level)
    for c in range(CHUNKS - 2, CHUNKS):
        reduce_chunk(c)

    summed = jnp.zeros((8, lanes), jnp.float32)
    for c in range(CHUNKS):
        d, r = spot(shot, c)
        held = total[d, pl.ds(r, piece)]
        summed = summed + jnp.sum((held * held).reshape(piece // 8, 8, lanes), axis=0)
    squares[me] = summed

    def square_copy(k):
        return pltpu.make_async_remote_copy(
            src_ref=squares.at[me],
            dst_ref=squares.at[me],
            send_sem=square_send.at[k - 1],
            recv_sem=square_recv.at[k - 1],
            device_id={"slab": lax.rem(me + k, slabs)},
            device_id_type=MESH,
        )

    def shot_copy(k):
        return pltpu.make_async_remote_copy(
            src_ref=sums.at[shot],
            dst_ref=sums.at[shot],
            send_sem=sum_send.at[k - 1],
            recv_sem=sum_recv.at[k - 1],
            device_id={"shot": lax.rem(shot + k, shots)},
            device_id_type=MESH,
        )

    for k in range(1, slabs):
        square_copy(k).start()

    def settle_parts(c, carry):
        wait_sent(stages - 1, c)
        for k in range(1, shots):
            part_copy(k, c).wait_send()
        return carry

    lax.fori_loop(0, CHUNKS, settle_parts, 0)
    for k in range(1, slabs):
        square_copy(k).wait_recv()
    everything = squares[0]
    for k in range(1, slabs):
        everything = everything + squares[k]
    sums[shot] = everything
    for k in range(1, shots):
        shot_copy(k).start()

    def settle(c, carry):
        for k in range(1, shots):
            whole_copy(k, c).wait()
        return carry

    lax.fori_loop(0, CHUNKS, settle, 0)
    store = pltpu.make_async_copy(total, total_out, load_sem.at[0])
    store.start()
    for k in range(1, slabs):
        square_copy(k).wait_send()
    for k in range(1, shots):
        shot_copy(k).wait()
    everything = sums[0]
    for k in range(1, shots):
        everything = everything + sums[k]
    cells = slabs * depth * width * lanes
    mean = jnp.sum(everything, keepdims=True) / cells + tiny_eps
    inv_out[...] = jnp.broadcast_to(1.0 / jnp.sqrt(mean), inv_out.shape)
    store.wait()


def finish(total, slowness, inverse, new_slowness, gradient):
    share = gradient.shape[1]
    first = pl.multiple_of(lax.axis_index("shot") * share, 8)
    inv = inverse[0:1]
    for d in range(total.shape[0]):
        new_slowness[d] = slowness[d] - update_rate * (total[d] * inv)
        gradient[d] = total[d, pl.ds(first, share)] * inv


def per_device(
    slowness,
    wave_prev,
    wave_now,
    memory,
    adjoint_now,
    adjoint_prev,
    wavelet,
    src_cells,
    src_signs,
    rec_cells,
    observed,
):
    depth, width, lanes = slowness.shape
    shots, slabs = lax.axis_size("shot"), lax.axis_size("slab")
    rows = width // CHUNKS
    piece = depth * rows // shots
    assert width % CHUNKS == 0 and rows % SUB == 0 and depth >= LINK
    assert depth * rows % shots == 0 and rows % piece == 0 and piece % 8 == 0
    receivers = rec_cells.shape[0]
    stages = 2 * STEPS - 1
    f32 = jnp.float32
    block = (depth, width, lanes)
    padded = (depth, width + 2 * PAD, lanes)
    anywhere = pl.BlockSpec(memory_space=pl.ANY)
    vmem = pl.BlockSpec(memory_space=pltpu.VMEM)
    dma = pltpu.SemaphoreType.DMA
    total, inverse = pl.pallas_call(
        functools.partial(kernel, shots, slabs),
        name="invert",
        out_shape=(
            jax.ShapeDtypeStruct(block, f32),
            jax.ShapeDtypeStruct((8, lanes), f32),
        ),
        in_specs=[anywhere] * 11,
        out_specs=(anywhere, vmem),
        scratch_shapes=[
            pltpu.VMEM(block, f32),
            pltpu.VMEM(block, f32),
            pltpu.VMEM((STEPS + 1, *padded), f32),
            pltpu.VMEM((MECH, *block), f32),
            pltpu.VMEM(block, f32),
            pltpu.VMEM(block, f32),
            pltpu.VMEM((STEPS - 1, *padded), f32),
            pltpu.VMEM((STEPS, *block), f32),
            pltpu.VMEM((STEPS, *block), f32),
            pltpu.VMEM((STEPS, *block), f32),
            pltpu.VMEM((STEPS - 1, *block), f32),
            pltpu.VMEM(block, f32),
            pltpu.VMEM(block, f32),
            pltpu.VMEM(block, f32),
            pltpu.VMEM(block, f32),
            pltpu.VMEM(block, f32),
            pltpu.VMEM((STEPS, *block), f32),
            pltpu.VMEM(block, f32),
            pltpu.VMEM((depth * width, receivers), jnp.bfloat16),
            pltpu.VMEM(((1 + 3 * STEPS) * lanes, receivers), jnp.bfloat16),
            pltpu.VMEM((stages, 2, LINK, width, lanes), f32),
            pltpu.VMEM(block, f32),
            pltpu.VMEM((CHUNKS, shots - 1, piece, lanes), f32),
            pltpu.VMEM(block, f32),
            pltpu.VMEM((slabs, 8, lanes), f32),
            pltpu.VMEM((shots, 8, lanes), f32),
            pltpu.SMEM(wavelet.shape, f32),
            pltpu.VMEM(src_cells.shape, jnp.int32),
            pltpu.VMEM(src_signs.shape, jnp.int32),
            pltpu.VMEM((1, receivers), jnp.int32),
            pltpu.VMEM(observed.shape, f32),
            dma((11,)),
            dma((stages, 2, CHUNKS)),
            dma((stages, 2, CHUNKS)),
            dma((CHUNKS, shots - 1)),
            dma((CHUNKS, shots - 1)),
            dma((CHUNKS, shots - 1)),
            dma((CHUNKS, shots - 1)),
            dma((slabs - 1,)),
            dma((slabs - 1,)),
            dma((shots - 1,)),
            dma((shots - 1,)),
        ],
        compiler_params=pltpu.CompilerParams(
            collective_id=0, has_side_effects=True, vmem_limit_bytes=60 * 2**20
        ),
    )(
        slowness,
        wave_prev,
        wave_now,
        memory,
        adjoint_now,
        adjoint_prev,
        wavelet,
        src_cells,
        src_signs,
        rec_cells.reshape(1, receivers),
        observed,
    )
    share = width // shots
    new_slowness, gradient = pl.pallas_call(
        finish,
        name="finish",
        out_shape=(
            jax.ShapeDtypeStruct(block, f32),
            jax.ShapeDtypeStruct((depth, share, lanes), f32),
        ),
        in_specs=[vmem] * 3,
        out_specs=(vmem, vmem),
        compiler_params=pltpu.CompilerParams(vmem_limit_bytes=60 * 2**20),
    )(total, slowness, inverse)
    return (new_slowness, gradient)


def solution(mesh):
    in_specs = (
        P(("groups", "slab"), None, None),
        P(("groups", "shot"), "slab", None, None),
        P(("groups", "shot"), "slab", None, None),
        P(("groups", "shot"), None, "slab", None, None),
        P(("groups", "shot"), "slab", None, None),
        P(("groups", "shot"), "slab", None, None),
        P(),
        P(("groups", "shot"), None),
        P(("groups", "shot"), None),
        P("groups"),
        P(("groups", "shot"), None, None),
    )
    out_specs = (P(("groups", "slab"), None, None), P(("groups", "slab"), "shot", None))
    return jax.shard_map(
        per_device, mesh=mesh, in_specs=in_specs, out_specs=out_specs, check_vma=False
    )
```

```python
import functools

import jax
import jax.numpy as jnp
from jax import lax
from jax.experimental import pallas as pl
from jax.experimental.pallas import tpu as pltpu
from jax.sharding import PartitionSpec as P

STEPS = 4
MECH = 3
LINK = 2
PAD = 8
CHUNKS = 4
WIDE = 2

center_coef = -2.5
near_coef = 4.0 / 3.0
far_coef = -1.0 / 12.0
courant = 0.14
relax_decay = (0.3, 0.7, 0.95)
relax_weight = (0.3, 0.2, 0.1)
update_rate = 0.05
tiny_eps = 1e-06

lag_weight = tuple(
    sum(w * a**j for w, a in zip(relax_weight, relax_decay)) for j in range(STEPS - 1)
)

MESH = pl.DeviceIdType.MESH


def contract_lanes(a, b):
    return lax.dot_general(a, b, (((1,), (1,)), ((), ())), preferred_element_type=jnp.float32)


def kernel(
    shots,
    slabs,
    slowness_in,
    prev_in,
    now_in,
    memory_in,
    adj_now_in,
    adj_prev_in,
    wavelet_in,
    src_cells_in,
    src_signs_in,
    rec_cells_in,
    observed_in,
    total_out,
    inv_out,
    slow,
    older,
    field,
    relax,
    adj_now,
    adj_prev,
    drive,
    united,
    saved,
    fading,
    curves,
    pushes,
    accum,
    scaled,
    factor,
    count,
    seen,
    source,
    hot_rows,
    pieces,
    halo,
    grad,
    parts,
    total,
    squares,
    sums,
    wavelet,
    src_cells,
    src_signs,
    rec_cells,
    observed,
    load_sem,
    halo_send,
    halo_recv,
    part_send,
    part_recv,
    whole_send,
    whole_recv,
    square_send,
    square_recv,
    sum_send,
    sum_recv,
):
    depth, width, lanes = slow.shape
    rows = width // CHUNKS
    stages = 2 * STEPS - 1
    cuts = [WIDE] * (stages - 1) + [CHUNKS]
    me = lax.axis_index("slab")
    shot = lax.axis_index("shot")

    loads = [
        pltpu.make_async_copy(now_in.at[0], field.at[0, :, PAD : PAD + width], load_sem.at[0]),
        pltpu.make_async_copy(slowness_in, slow, load_sem.at[1]),
        pltpu.make_async_copy(memory_in.at[0], relax, load_sem.at[2]),
        pltpu.make_async_copy(prev_in.at[0], older, load_sem.at[3]),
        pltpu.make_async_copy(adj_now_in.at[0], adj_now, load_sem.at[4]),
        pltpu.make_async_copy(adj_prev_in.at[0], adj_prev, load_sem.at[5]),
        pltpu.make_async_copy(wavelet_in, wavelet, load_sem.at[6]),
        pltpu.make_async_copy(src_cells_in, src_cells, load_sem.at[7]),
        pltpu.make_async_copy(src_signs_in, src_signs, load_sem.at[8]),
        pltpu.make_async_copy(rec_cells_in, rec_cells, load_sem.at[9]),
        pltpu.make_async_copy(observed_in, observed, load_sem.at[10]),
    ]
    barrier = pltpu.get_barrier_semaphore()
    for k in range(1, slabs):
        pl.semaphore_signal(
            barrier, inc=1, device_id={"slab": lax.rem(me + k, slabs)}, device_id_type=MESH
        )
    for k in range(1, shots):
        pl.semaphore_signal(
            barrier, inc=1, device_id={"shot": lax.rem(shot + k, shots)}, device_id_type=MESH
        )
    for copy in loads:
        copy.start()
    pl.semaphore_wait(barrier, slabs - 1 + shots - 1)

    def outgoing(stage, side, c):
        first = depth - LINK if side == 0 else 0
        planes = pl.ds(first, LINK)
        span = width // cuts[stage]
        start = pl.multiple_of(c * span, 8)
        if stage == 0:
            src = now_in.at[0, planes, pl.ds(start, span)]
        elif stage < STEPS:
            src = field.at[stage, planes, pl.ds(start + PAD, span)]
        else:
            src = drive.at[stage - STEPS, planes, pl.ds(start + PAD, span)]
        target = me + 1 if side == 0 else me - 1
        return pltpu.make_async_remote_copy(
            src_ref=src,
            dst_ref=halo.at[stage, side, :, pl.ds(start, span)],
            send_sem=halo_send.at[stage, side, c],
            recv_sem=halo_recv.at[stage, side, c],
            device_id={"slab": target},
            device_id_type=MESH,
        )

    has_up = me < slabs - 1
    has_down = me > 0

    def send_after(stage, c):
        ratio = cuts[stage + 1] // cuts[stage]
        for k in range(ratio):
            send_halo(stage + 1, c * ratio + k)

    def send_halo(stage, c):
        @pl.when(has_up)
        def _():
            outgoing(stage, 0, c).start()

        @pl.when(has_down)
        def _():
            outgoing(stage, 1, c).start()

    def wait_sent(stage, c):
        @pl.when(has_up)
        def _():
            outgoing(stage, 0, c).wait_send()

        @pl.when(has_down)
        def _():
            outgoing(stage, 1, c).wait_send()

    def wait_halo(stage, c):
        @pl.when(has_down)
        def _():
            outgoing(stage, 0, c).wait_recv()

        @pl.when(has_up)
        def _():
            outgoing(stage, 1, c).wait_recv()

    for c in range(cuts[0]):
        send_halo(0, c)

    @pl.when(jnp.logical_not(has_down))
    def _():
        halo[:, 0] = jnp.zeros((stages, LINK, width, lanes), jnp.float32)

    @pl.when(jnp.logical_not(has_up))
    def _():
        halo[:, 1] = jnp.zeros((stages, LINK, width, lanes), jnp.float32)

    edge = jnp.zeros((depth, PAD, lanes), jnp.float32)
    for n in range(STEPS):
        field[n, :, :PAD] = edge
        field[n, :, PAD + width :] = edge
    for n in range(STEPS - 1):
        drive[n, :, :PAD] = edge
        drive[n, :, PAD + width :] = edge

    def one_hot(index, height):
        at = lax.broadcasted_iota(jnp.int32, (height, index.shape[1]), 0)
        return jnp.where(at == index, 1.0, 0.0)

    first_row = me * (depth * width)
    for k in range(6, 11):
        loads[k].wait()
    src = src_cells[...]
    src_row = lax.div(src, lanes)
    src_lane = src - src_row * lanes
    src_at = (one_hot(src_lane, lanes) * src_signs[...].astype(jnp.float32)).astype(jnp.bfloat16)
    src_rows = one_hot(src_row - first_row, depth * width).astype(jnp.bfloat16)
    source[...] = contract_lanes(src_rows, src_at).reshape(depth, width, lanes)

    def place_receivers():
        rec = rec_cells[...]
        rec_row = lax.div(rec, lanes)
        rec_lane = rec - rec_row * lanes
        at_lane = one_hot(rec_lane, lanes)
        pieces[0:lanes] = at_lane.astype(jnp.bfloat16)
        for n in range(STEPS):
            rest = at_lane * observed[0, n : n + 1, :]
            for k in range(3):
                part = rest.astype(jnp.bfloat16)
                begin = (1 + 3 * n + k) * lanes
                pieces[begin : begin + lanes] = part
                rest = rest - part.astype(jnp.float32)
        hot_rows[...] = one_hot(rec_row - first_row, depth * width).astype(jnp.bfloat16)
        count[...] = contract_lanes(hot_rows[...], pieces[0:lanes]).reshape(depth, width, lanes)

    def place_observed(n):
        begin = (1 + 3 * n) * lanes
        got = contract_lanes(hot_rows[...], pieces[begin : begin + 3 * lanes])
        got = (got[:, 2 * lanes :] + got[:, lanes : 2 * lanes]) + got[:, :lanes]
        seen[n] = got.reshape(depth, width, lanes)

    loads[1].wait()
    for d in range(depth):
        s = slow[d]
        held = courant / (s * s)
        scaled[d] = held
        factor[d] = (-2.0 * held) / s
    loads[2].wait()

    def fade(k, carry):
        at = pl.ds(pl.multiple_of(k * 24, 8), 24)
        for d in range(depth):
            held = [relax[m, d, at] for m in range(MECH)]
            for n in range(STEPS):
                fading[n, d, at] = (held[0] + held[1]) + held[2]
                held = [relax_decay[m] * held[m] for m in range(MECH)]
        return carry

    lax.fori_loop(0, width // 24, fade, 0)
    for k in (0, 3, 4, 5):
        loads[k].wait()

    lane = lax.broadcasted_iota(jnp.int32, (8, lanes), 1)[:1]
    left_1 = jnp.where(lane >= 1, near_coef, 0.0)
    left_2 = jnp.where(lane >= 2, far_coef, 0.0)
    right_1 = jnp.where(lane < lanes - 1, near_coef, 0.0)
    right_2 = jnp.where(lane < lanes - 2, far_coef, 0.0)

    def laplace(ref, n, stage, r, size):
        def rows_at(d, shift):
            return ref[n, d, pl.ds(r + PAD + shift, size)]

        low = [halo[stage, 0, k, pl.ds(r, size)] for k in range(LINK)]
        mids = [rows_at(d, 0) for d in range(depth)]
        high = [halo[stage, 1, k, pl.ds(r, size)] for k in range(LINK)]
        planes = low + mids + high
        curved = []
        for d in range(depth):
            mid = mids[d]
            near = (planes[d + 1] + planes[d + 3]) + (rows_at(d, -1) + rows_at(d, 1))
            far = (planes[d] + planes[d + 4]) + (rows_at(d, -2) + rows_at(d, 2))
            along = (
                left_1 * pltpu.roll(mid, 1, 1)
                + right_1 * pltpu.roll(mid, lanes - 1, 1)
                + left_2 * pltpu.roll(mid, 2, 1)
                + right_2 * pltpu.roll(mid, lanes - 2, 1)
            )
            curved.append(
                (3.0 * center_coef) * mid + near_coef * near + far_coef * far + along
            )
        return curved, mids

    def blocks(stage, c, body):
        span = width // cuts[stage]
        size = 32 if span % 32 == 0 else 24 if span % 24 == 0 else 8
        for k in range(span // size):
            body(pl.multiple_of(c * span + k * size, 8), size)

    def adjoint_part(level, d, r, size, back, begin_accum):
        at = pl.ds(r, size)
        inner = pl.ds(r + PAD, size)
        up = back + (
            count[d, at] * field[level + 1, d, inner] - seen[level, d, at]
        )
        term = up * saved[level, d, at]
        term = term if begin_accum else accum[d, at] + term
        if level == 0:
            grad[d, at] = term * factor[d, at]
            return
        accum[d, at] = term
        united[level, d, at] = up
        pushed = scaled[d, at] * up
        out = pushed
        if level == STEPS - 2:
            pushes[d, at] = pushed
            out = pushed - lag_weight[0] * drive[0, d, inner]
        elif level == STEPS - 3:
            out = (pushed - lag_weight[0] * pushes[d, at]) - lag_weight[1] * drive[
                0, d, inner
            ]
        drive[STEPS - 1 - level, d, inner] = out

    def forward_stage(n):
        amount = wavelet[n]

        def chunk(c, carry):
            wait_halo(n, c)

            def body(r, size):
                at = pl.ds(r, size)
                inner = pl.ds(r + PAD, size)
                curved, mids = laplace(field, n, n, r, size)
                for d in range(depth):
                    accel = curved[d] + fading[n, d, at]
                    for m in range(n):
                        accel = accel - lag_weight[n - 1 - m] * curves[m, d, at]
                    before = older[d, at] if n == 0 else field[n - 1, d, inner]
                    newer = (2.0 * mids[d] - before) + scaled[d, at] * accel
                    newer = newer + amount * source[d, at]
                    saved[n, d, at] = accel
                    field[n + 1, d, inner] = newer
                    if n < STEPS - 1:
                        curves[n, d, at] = curved[d]
                    else:
                        adjoint_part(n, d, r, size, adj_now[d, at], True)

            blocks(n, c, body)
            send_after(n, c)
            return carry

        lax.fori_loop(0, cuts[n], chunk, 0)

    piece = depth * rows // shots

    def spot(owner, c):
        begin = owner * piece
        return begin // rows, pl.multiple_of(c * rows + begin % rows, 8)

    def part_copy(k, c):
        target = lax.rem(shot + k, shots)
        d, r = spot(target, c)
        return pltpu.make_async_remote_copy(
            src_ref=grad.at[d, pl.ds(r, piece)],
            dst_ref=parts.at[c, k - 1],
            send_sem=part_send.at[c, k - 1],
            recv_sem=part_recv.at[c, k - 1],
            device_id={"shot": target},
            device_id_type=MESH,
        )

    def whole_copy(k, c):
        target = lax.rem(shot + k, shots)
        d, r = spot(shot, c)
        return pltpu.make_async_remote_copy(
            src_ref=total.at[d, pl.ds(r, piece)],
            dst_ref=total.at[d, pl.ds(r, piece)],
            send_sem=whole_send.at[c, k - 1],
            recv_sem=whole_recv.at[c, k - 1],
            device_id={"shot": target},
            device_id_type=MESH,
        )

    def reduce_chunk(c):
        d, r = spot(shot, c)
        held = grad[d, pl.ds(r, piece)]
        for k in range(1, shots):
            part_copy(k, c).wait_recv()
            held = held + parts[c, k - 1]
        total[d, pl.ds(r, piece)] = held
        for k in range(1, shots):
            whole_copy(k, c).start()

    def backward_stage(level):
        stage = 2 * STEPS - 2 - level

        def chunk(c, carry):
            wait_halo(stage, c)

            def body(r, size):
                at = pl.ds(r, size)
                curved, _ = laplace(drive, stage - STEPS, stage, r, size)
                for d in range(depth):
                    after = united[level + 1, d, at]
                    if level == STEPS - 2:
                        base = adj_prev[d, at]
                    else:
                        base = -united[level + 2, d, at]
                    adjoint_part(level, d, r, size, (base + 2.0 * after) + curved[d], False)

            blocks(stage, c, body)
            if level > 0:
                send_after(stage, c)
            else:
                for k in range(1, shots):
                    part_copy(k, c).start()

                @pl.when(c >= 2)
                def _():
                    reduce_chunk(c - 2)

            return carry

        lax.fori_loop(0, cuts[stage], chunk, 0)

    for n in range(STEPS):
        forward_stage(n)
        if n == 0:
            place_receivers()
        if n in (1, 2):
            for k in (2 * n - 2, 2 * n - 1):
                place_observed(k)
    for level in reversed(range(STEPS - 1)):
        backward_stage(level)
    for c in range(CHUNKS - 2, CHUNKS):
        reduce_chunk(c)

    summed = jnp.zeros((8, lanes), jnp.float32)
    for c in range(CHUNKS):
        d, r = spot(shot, c)
        held = total[d, pl.ds(r, piece)]
        summed = summed + jnp.sum((held * held).reshape(piece // 8, 8, lanes), axis=0)
    squares[me] = summed

    def square_copy(k):
        return pltpu.make_async_remote_copy(
            src_ref=squares.at[me],
            dst_ref=squares.at[me],
            send_sem=square_send.at[k - 1],
            recv_sem=square_recv.at[k - 1],
            device_id={"slab": lax.rem(me + k, slabs)},
            device_id_type=MESH,
        )

    def shot_copy(k):
        return pltpu.make_async_remote_copy(
            src_ref=sums.at[shot],
            dst_ref=sums.at[shot],
            send_sem=sum_send.at[k - 1],
            recv_sem=sum_recv.at[k - 1],
            device_id={"shot": lax.rem(shot + k, shots)},
            device_id_type=MESH,
        )

    for k in range(1, slabs):
        square_copy(k).start()

    def settle_parts(c, carry):
        for k in range(1, shots):
            part_copy(k, c).wait_send()
        return carry

    lax.fori_loop(0, CHUNKS, settle_parts, 0)
    for stage in range(stages):
        for c in range(cuts[stage]):
            wait_sent(stage, c)
    for k in range(1, slabs):
        square_copy(k).wait_recv()
    everything = squares[0]
    for k in range(1, slabs):
        everything = everything + squares[k]
    sums[shot] = everything
    for k in range(1, shots):
        shot_copy(k).start()

    def settle(c, carry):
        for k in range(1, shots):
            whole_copy(k, c).wait()
        return carry

    lax.fori_loop(0, CHUNKS, settle, 0)
    store = pltpu.make_async_copy(total, total_out, load_sem.at[0])
    store.start()
    for k in range(1, slabs):
        square_copy(k).wait_send()
    for k in range(1, shots):
        shot_copy(k).wait()
    everything = sums[0]
    for k in range(1, shots):
        everything = everything + sums[k]
    cells = slabs * depth * width * lanes
    mean = jnp.sum(everything, keepdims=True) / cells + tiny_eps
    inv_out[...] = jnp.broadcast_to(1.0 / jnp.sqrt(mean), inv_out.shape)
    store.wait()


def finish(
    total_in,
    slowness_in,
    inverse_in,
    new_slowness_out,
    gradient_out,
    total,
    slowness,
    inverse,
    new_slowness,
    gradient,
    scale_sem,
    total_sem,
    slow_sem,
    new_sem,
    grad_sem,
):
    depth, share = gradient.shape[:2]
    first = pl.multiple_of(lax.axis_index("shot") * share, 8)
    scale = pltpu.make_async_copy(inverse_in, inverse, scale_sem)
    scale.start()
    loads = []
    for d in range(depth):
        loads.append(
            (
                pltpu.make_async_copy(total_in.at[d], total.at[d], total_sem.at[d]),
                pltpu.make_async_copy(slowness_in.at[d], slowness.at[d], slow_sem.at[d]),
            )
        )
        for copy in loads[d]:
            copy.start()
    scale.wait()
    inv = inverse[0:1]
    stores = []
    for d in range(depth):
        for copy in loads[d]:
            copy.wait()
        new_slowness[d] = slowness[d] - update_rate * (total[d] * inv)
        gradient[d] = total[d, pl.ds(first, share)] * inv
        stores.append(pltpu.make_async_copy(new_slowness.at[d], new_slowness_out.at[d], new_sem.at[d]))
        stores.append(pltpu.make_async_copy(gradient.at[d], gradient_out.at[d], grad_sem.at[d]))
        for copy in stores[-2:]:
            copy.start()
    for copy in stores:
        copy.wait()


def per_device(
    slowness,
    wave_prev,
    wave_now,
    memory,
    adjoint_now,
    adjoint_prev,
    wavelet,
    src_cells,
    src_signs,
    rec_cells,
    observed,
):
    depth, width, lanes = slowness.shape
    shots, slabs = lax.axis_size("shot"), lax.axis_size("slab")
    rows = width // CHUNKS
    piece = depth * rows // shots
    assert width % 96 == 0 and depth >= LINK
    assert depth * rows % shots == 0 and rows % piece == 0 and piece % 8 == 0
    receivers = rec_cells.shape[0]
    stages = 2 * STEPS - 1
    f32 = jnp.float32
    block = (depth, width, lanes)
    padded = (depth, width + 2 * PAD, lanes)
    anywhere = pl.BlockSpec(memory_space=pl.ANY)
    vmem = pl.BlockSpec(memory_space=pltpu.VMEM)
    dma = pltpu.SemaphoreType.DMA
    total, inverse = pl.pallas_call(
        functools.partial(kernel, shots, slabs),
        name="invert",
        out_shape=(
            jax.ShapeDtypeStruct(block, f32),
            jax.ShapeDtypeStruct((8, lanes), f32),
        ),
        in_specs=[anywhere] * 11,
        out_specs=(anywhere, vmem),
        scratch_shapes=[
            pltpu.VMEM(block, f32),
            pltpu.VMEM(block, f32),
            pltpu.VMEM((STEPS + 1, *padded), f32),
            pltpu.VMEM((MECH, *block), f32),
            pltpu.VMEM(block, f32),
            pltpu.VMEM(block, f32),
            pltpu.VMEM((STEPS - 1, *padded), f32),
            pltpu.VMEM((STEPS, *block), f32),
            pltpu.VMEM((STEPS, *block), f32),
            pltpu.VMEM((STEPS, *block), f32),
            pltpu.VMEM((STEPS - 1, *block), f32),
            pltpu.VMEM(block, f32),
            pltpu.VMEM(block, f32),
            pltpu.VMEM(block, f32),
            pltpu.VMEM(block, f32),
            pltpu.VMEM(block, f32),
            pltpu.VMEM((STEPS, *block), f32),
            pltpu.VMEM(block, f32),
            pltpu.VMEM((depth * width, receivers), jnp.bfloat16),
            pltpu.VMEM(((1 + 3 * STEPS) * lanes, receivers), jnp.bfloat16),
            pltpu.VMEM((stages, 2, LINK, width, lanes), f32),
            pltpu.VMEM(block, f32),
            pltpu.VMEM((CHUNKS, shots - 1, piece, lanes), f32),
            pltpu.VMEM(block, f32),
            pltpu.VMEM((slabs, 8, lanes), f32),
            pltpu.VMEM((shots, 8, lanes), f32),
            pltpu.SMEM(wavelet.shape, f32),
            pltpu.VMEM(src_cells.shape, jnp.int32),
            pltpu.VMEM(src_signs.shape, jnp.int32),
            pltpu.VMEM((1, receivers), jnp.int32),
            pltpu.VMEM(observed.shape, f32),
            dma((11,)),
            dma((stages, 2, CHUNKS)),
            dma((stages, 2, CHUNKS)),
            dma((CHUNKS, shots - 1)),
            dma((CHUNKS, shots - 1)),
            dma((CHUNKS, shots - 1)),
            dma((CHUNKS, shots - 1)),
            dma((slabs - 1,)),
            dma((slabs - 1,)),
            dma((shots - 1,)),
            dma((shots - 1,)),
        ],
        compiler_params=pltpu.CompilerParams(
            collective_id=0, has_side_effects=True, vmem_limit_bytes=60 * 2**20
        ),
    )(
        slowness,
        wave_prev,
        wave_now,
        memory,
        adjoint_now,
        adjoint_prev,
        wavelet,
        src_cells,
        src_signs,
        rec_cells.reshape(1, receivers),
        observed,
    )
    share = width // shots
    new_slowness, gradient = pl.pallas_call(
        finish,
        name="finish",
        out_shape=(
            jax.ShapeDtypeStruct(block, f32),
            jax.ShapeDtypeStruct((depth, share, lanes), f32),
        ),
        in_specs=[anywhere] * 3,
        out_specs=(anywhere, anywhere),
        scratch_shapes=[
            pltpu.VMEM(block, f32),
            pltpu.VMEM(block, f32),
            pltpu.VMEM((8, lanes), f32),
            pltpu.VMEM(block, f32),
            pltpu.VMEM((depth, share, lanes), f32),
            dma(()),
            dma((depth,)),
            dma((depth,)),
            dma((depth,)),
            dma((depth,)),
        ],
        compiler_params=pltpu.CompilerParams(vmem_limit_bytes=60 * 2**20),
    )(total, slowness, inverse)
    return (new_slowness, gradient)


def solution(mesh):
    in_specs = (
        P(("groups", "slab"), None, None),
        P(("groups", "shot"), "slab", None, None),
        P(("groups", "shot"), "slab", None, None),
        P(("groups", "shot"), None, "slab", None, None),
        P(("groups", "shot"), "slab", None, None),
        P(("groups", "shot"), "slab", None, None),
        P(),
        P(("groups", "shot"), None),
        P(("groups", "shot"), None),
        P("groups"),
        P(("groups", "shot"), None, None),
    )
    out_specs = (P(("groups", "slab"), None, None), P(("groups", "slab"), "shot", None))
    return jax.shard_map(
        per_device, mesh=mesh, in_specs=in_specs, out_specs=out_specs, check_vma=False
    )
```

```python
import functools

import jax
import jax.numpy as jnp
from jax import lax
from jax.experimental import pallas as pl
from jax.experimental.pallas import tpu as pltpu
from jax.sharding import PartitionSpec as P

STEPS = 4
MECH = 3
LINK = 2
PAD = 8
CHUNKS = 6
LAG = 4
WIDE = 3

center_coef = -2.5
near_coef = 4.0 / 3.0
far_coef = -1.0 / 12.0
courant = 0.14
relax_decay = (0.3, 0.7, 0.95)
relax_weight = (0.3, 0.2, 0.1)
update_rate = 0.05
tiny_eps = 1e-06

lag_weight = tuple(
    sum(w * a**j for w, a in zip(relax_weight, relax_decay)) for j in range(STEPS - 1)
)

MESH = pl.DeviceIdType.MESH


def contract_lanes(a, b):
    return lax.dot_general(a, b, (((1,), (1,)), ((), ())), preferred_element_type=jnp.float32)


def kernel(
    shots,
    slabs,
    slowness_in,
    prev_in,
    now_in,
    memory_in,
    adj_now_in,
    adj_prev_in,
    wavelet_in,
    src_cells_in,
    src_signs_in,
    rec_cells_in,
    observed_in,
    total_out,
    inv_out,
    slow,
    older,
    field,
    relax,
    adj_now,
    adj_prev,
    drive,
    united,
    saved,
    fading,
    curves,
    pushes,
    accum,
    scaled,
    factor,
    count,
    seen,
    source,
    hot_rows,
    pieces,
    halo,
    grad,
    parts,
    total,
    squares,
    wavelet,
    src_cells,
    src_signs,
    rec_cells,
    observed,
    load_sem,
    halo_send,
    halo_recv,
    part_send,
    part_recv,
    whole_send,
    whole_recv,
    square_send,
    square_recv,
):
    depth, width, lanes = slow.shape
    rows = width // CHUNKS
    stages = 2 * STEPS - 1
    cuts = [WIDE] * (stages - 1) + [CHUNKS]
    me = lax.axis_index("slab")
    shot = lax.axis_index("shot")

    loads = [
        pltpu.make_async_copy(now_in.at[0], field.at[0, :, PAD : PAD + width], load_sem.at[0]),
        pltpu.make_async_copy(slowness_in, slow, load_sem.at[1]),
        pltpu.make_async_copy(memory_in.at[0], relax, load_sem.at[2]),
        pltpu.make_async_copy(prev_in.at[0], older, load_sem.at[3]),
        pltpu.make_async_copy(adj_now_in.at[0], adj_now, load_sem.at[4]),
        pltpu.make_async_copy(adj_prev_in.at[0], adj_prev, load_sem.at[5]),
        pltpu.make_async_copy(wavelet_in, wavelet, load_sem.at[6]),
        pltpu.make_async_copy(src_cells_in, src_cells, load_sem.at[7]),
        pltpu.make_async_copy(src_signs_in, src_signs, load_sem.at[8]),
        pltpu.make_async_copy(rec_cells_in, rec_cells, load_sem.at[9]),
        pltpu.make_async_copy(observed_in, observed, load_sem.at[10]),
    ]
    barrier = pltpu.get_barrier_semaphore()
    team = shots * slabs
    place = me * shots + shot

    def member(k):
        other = lax.rem(place + k, team)
        return {"slab": other // shots, "shot": lax.rem(other, shots)}

    def greet(k, carry):
        pl.semaphore_signal(barrier, inc=1, device_id=member(k), device_id_type=MESH)
        return carry

    lax.fori_loop(1, team, greet, 0)
    for copy in loads:
        copy.start()
    pl.semaphore_wait(barrier, team - 1)

    def outgoing(stage, side, c):
        first = depth - LINK if side == 0 else 0
        planes = pl.ds(first, LINK)
        span = width // cuts[stage]
        start = pl.multiple_of(c * span, 8)
        if stage == 0:
            src = now_in.at[0, planes, pl.ds(start, span)]
        elif stage < STEPS:
            src = field.at[stage, planes, pl.ds(start + PAD, span)]
        else:
            src = drive.at[stage - STEPS, planes, pl.ds(start + PAD, span)]
        target = me + 1 if side == 0 else me - 1
        return pltpu.make_async_remote_copy(
            src_ref=src,
            dst_ref=halo.at[stage, side, :, pl.ds(start, span)],
            send_sem=halo_send.at[stage, side, c],
            recv_sem=halo_recv.at[stage, side, c],
            device_id={"slab": target},
            device_id_type=MESH,
        )

    has_up = me < slabs - 1
    has_down = me > 0

    def send_after(stage, c):
        ratio = cuts[stage + 1] // cuts[stage]
        for k in range(ratio):
            send_halo(stage + 1, c * ratio + k)

    def send_halo(stage, c):
        @pl.when(has_up)
        def _():
            outgoing(stage, 0, c).start()

        @pl.when(has_down)
        def _():
            outgoing(stage, 1, c).start()

    def wait_sent(stage, c):
        @pl.when(has_up)
        def _():
            outgoing(stage, 0, c).wait_send()

        @pl.when(has_down)
        def _():
            outgoing(stage, 1, c).wait_send()

    def wait_halo(stage, c):
        @pl.when(has_down)
        def _():
            outgoing(stage, 0, c).wait_recv()

        @pl.when(has_up)
        def _():
            outgoing(stage, 1, c).wait_recv()

    for c in range(cuts[0]):
        send_halo(0, c)

    @pl.when(jnp.logical_not(has_down))
    def _():
        halo[:, 0] = jnp.zeros((stages, LINK, width, lanes), jnp.float32)

    @pl.when(jnp.logical_not(has_up))
    def _():
        halo[:, 1] = jnp.zeros((stages, LINK, width, lanes), jnp.float32)

    edge = jnp.zeros((depth, PAD, lanes), jnp.float32)
    for n in range(STEPS):
        field[n, :, :PAD] = edge
        field[n, :, PAD + width :] = edge
    for n in range(STEPS - 1):
        drive[n, :, :PAD] = edge
        drive[n, :, PAD + width :] = edge

    def one_hot(index, height):
        at = lax.broadcasted_iota(jnp.int32, (height, index.shape[1]), 0)
        return jnp.where(at == index, 1.0, 0.0)

    first_row = me * (depth * width)
    for k in range(6, 11):
        loads[k].wait()
    src = src_cells[...]
    src_row = lax.div(src, lanes)
    src_lane = src - src_row * lanes
    src_at = (one_hot(src_lane, lanes) * src_signs[...].astype(jnp.float32)).astype(jnp.bfloat16)
    src_rows = one_hot(src_row - first_row, depth * width).astype(jnp.bfloat16)
    source[...] = contract_lanes(src_rows, src_at).reshape(depth, width, lanes)

    def place_receivers():
        rec = rec_cells[...]
        rec_row = lax.div(rec, lanes)
        rec_lane = rec - rec_row * lanes
        at_lane = one_hot(rec_lane, lanes)
        pieces[0:lanes] = at_lane.astype(jnp.bfloat16)
        for n in range(STEPS):
            rest = at_lane * observed[0, n : n + 1, :]
            for k in range(3):
                part = rest.astype(jnp.bfloat16)
                begin = (1 + 3 * n + k) * lanes
                pieces[begin : begin + lanes] = part
                rest = rest - part.astype(jnp.float32)
        hot_rows[...] = one_hot(rec_row - first_row, depth * width).astype(jnp.bfloat16)
        count[...] = contract_lanes(hot_rows[...], pieces[0:lanes]).reshape(depth, width, lanes)

    def place_observed(n, part, parts_of):
        height = depth * width // parts_of
        at = pl.ds(pl.multiple_of(part * height, 16), height)
        begin = (1 + 3 * n) * lanes
        got = contract_lanes(hot_rows[at], pieces[begin : begin + 3 * lanes])
        seen[n, at] = (got[:, 2 * lanes :] + got[:, lanes : 2 * lanes]) + got[:, :lanes]

    loads[1].wait()
    for d in range(depth):
        s = slow[d]
        held = courant / (s * s)
        scaled[d] = held
        factor[d] = (-2.0 * held) / s
    loads[2].wait()

    def fade(k, carry):
        at = pl.ds(pl.multiple_of(k * 24, 8), 24)
        for d in range(depth):
            held = [relax[m, d, at] for m in range(MECH)]
            for n in range(STEPS):
                fading[n, d, at] = (held[0] + held[1]) + held[2]
                held = [relax_decay[m] * held[m] for m in range(MECH)]
        return carry

    lax.fori_loop(0, width // 24, fade, 0)
    place_receivers()
    place_observed(STEPS - 1, 0, 1)
    for k in (0, 3, 4, 5):
        loads[k].wait()

    lane = lax.broadcasted_iota(jnp.int32, (8, lanes), 1)[:1]
    left_1 = jnp.where(lane >= 1, near_coef, 0.0)
    left_2 = jnp.where(lane >= 2, far_coef, 0.0)
    right_1 = jnp.where(lane < lanes - 1, near_coef, 0.0)
    right_2 = jnp.where(lane < lanes - 2, far_coef, 0.0)

    def laplace(ref, n, stage, r, size):
        def rows_at(d, shift):
            return ref[n, d, pl.ds(r + PAD + shift, size)]

        low = [halo[stage, 0, k, pl.ds(r, size)] for k in range(LINK)]
        mids = [rows_at(d, 0) for d in range(depth)]
        high = [halo[stage, 1, k, pl.ds(r, size)] for k in range(LINK)]
        planes = low + mids + high
        curved = []
        for d in range(depth):
            mid = mids[d]
            near = (planes[d + 1] + planes[d + 3]) + (rows_at(d, -1) + rows_at(d, 1))
            far = (planes[d] + planes[d + 4]) + (rows_at(d, -2) + rows_at(d, 2))
            along = (
                left_1 * pltpu.roll(mid, 1, 1)
                + right_1 * pltpu.roll(mid, lanes - 1, 1)
                + left_2 * pltpu.roll(mid, 2, 1)
                + right_2 * pltpu.roll(mid, lanes - 2, 1)
            )
            curved.append(
                (3.0 * center_coef) * mid + near_coef * near + far_coef * far + along
            )
        return curved, mids

    def blocks(stage, c, body):
        span = width // cuts[stage]
        size = 32 if span % 32 == 0 else 24 if span % 24 == 0 else 8
        for k in range(span // size):
            body(pl.multiple_of(c * span + k * size, 8), size)

    def adjoint_part(level, d, r, size, back, begin_accum):
        at = pl.ds(r, size)
        inner = pl.ds(r + PAD, size)
        up = back + (
            count[d, at] * field[level + 1, d, inner] - seen[level, pl.ds(d * width + r, size)]
        )
        term = up * saved[level, d, at]
        term = term if begin_accum else accum[d, at] + term
        if level == 0:
            grad[d, at] = term * factor[d, at]
            return
        accum[d, at] = term
        united[level, d, at] = up
        pushed = scaled[d, at] * up
        out = pushed
        if level == STEPS - 2:
            pushes[d, at] = pushed
            out = pushed - lag_weight[0] * drive[0, d, inner]
        elif level == STEPS - 3:
            out = (pushed - lag_weight[0] * pushes[d, at]) - lag_weight[1] * drive[
                0, d, inner
            ]
        drive[STEPS - 1 - level, d, inner] = out

    def forward_stage(n):
        amount = wavelet[n]

        def chunk(c, carry):
            wait_halo(n, c)

            def body(r, size):
                at = pl.ds(r, size)
                inner = pl.ds(r + PAD, size)
                curved, mids = laplace(field, n, n, r, size)
                for d in range(depth):
                    accel = curved[d] + fading[n, d, at]
                    for m in range(n):
                        accel = accel - lag_weight[n - 1 - m] * curves[m, d, at]
                    before = older[d, at] if n == 0 else field[n - 1, d, inner]
                    newer = (2.0 * mids[d] - before) + scaled[d, at] * accel
                    newer = newer + amount * source[d, at]
                    saved[n, d, at] = accel
                    field[n + 1, d, inner] = newer
                    if n < STEPS - 1:
                        curves[n, d, at] = curved[d]
                    else:
                        adjoint_part(n, d, r, size, adj_now[d, at], True)

            blocks(n, c, body)
            send_after(n, c)
            if n < STEPS - 1:
                place_observed(STEPS - 2 - n, c, cuts[n])
            return carry

        lax.fori_loop(0, cuts[n], chunk, 0)

    piece = depth * rows // shots

    def spot(owner, c):
        begin = owner * piece
        return begin // rows, pl.multiple_of(c * rows + begin % rows, 8)

    def part_copy(k, c):
        target = lax.rem(shot + k, shots)
        d, r = spot(target, c)
        return pltpu.make_async_remote_copy(
            src_ref=grad.at[d, pl.ds(r, piece)],
            dst_ref=parts.at[c, k - 1],
            send_sem=part_send.at[c, k - 1],
            recv_sem=part_recv.at[c, k - 1],
            device_id={"shot": target},
            device_id_type=MESH,
        )

    def whole_copy(k, c):
        target = lax.rem(shot + k, shots)
        d, r = spot(shot, c)
        return pltpu.make_async_remote_copy(
            src_ref=total.at[d, pl.ds(r, piece)],
            dst_ref=total.at[d, pl.ds(r, piece)],
            send_sem=whole_send.at[c, k - 1],
            recv_sem=whole_recv.at[c, k - 1],
            device_id={"shot": target},
            device_id_type=MESH,
        )

    def reduce_chunk(c):
        d, r = spot(shot, c)
        held = grad[d, pl.ds(r, piece)]
        for k in range(1, shots):
            part_copy(k, c).wait_recv()
            held = held + parts[c, k - 1]
        total[d, pl.ds(r, piece)] = held
        for k in range(1, shots):
            whole_copy(k, c).start()

    def backward_stage(level):
        stage = 2 * STEPS - 2 - level

        def chunk(c, carry):
            wait_halo(stage, c)

            def body(r, size):
                at = pl.ds(r, size)
                curved, _ = laplace(drive, stage - STEPS, stage, r, size)
                for d in range(depth):
                    after = united[level + 1, d, at]
                    if level == STEPS - 2:
                        base = adj_prev[d, at]
                    else:
                        base = -united[level + 2, d, at]
                    adjoint_part(level, d, r, size, (base + 2.0 * after) + curved[d], False)

            blocks(stage, c, body)
            if level > 0:
                send_after(stage, c)
            else:
                for k in range(1, shots):
                    part_copy(k, c).start()

                @pl.when(c >= LAG)
                def _():
                    reduce_chunk(c - LAG)

            return carry

        lax.fori_loop(0, cuts[stage], chunk, 0)

    for n in range(STEPS):
        forward_stage(n)
    for level in reversed(range(STEPS - 1)):
        backward_stage(level)
    for c in range(CHUNKS - LAG, CHUNKS):
        reduce_chunk(c)

    summed = jnp.zeros((8, lanes), jnp.float32)
    for c in range(CHUNKS):
        d, r = spot(shot, c)
        held = total[d, pl.ds(r, piece)]
        summed = summed + jnp.sum((held * held).reshape(piece // 8, 8, lanes), axis=0)
    squares[place] = summed

    def square_copy(k):
        return pltpu.make_async_remote_copy(
            src_ref=squares.at[place],
            dst_ref=squares.at[place],
            send_sem=square_send.at[k - 1],
            recv_sem=square_recv.at[k - 1],
            device_id=member(k),
            device_id_type=MESH,
        )

    def tell(k, carry):
        square_copy(k).start()
        return carry

    lax.fori_loop(1, team, tell, 0)

    def settle_parts(c, carry):
        for k in range(1, shots):
            part_copy(k, c).wait_send()
        return carry

    lax.fori_loop(0, CHUNKS, settle_parts, 0)
    for stage in range(stages):
        for c in range(cuts[stage]):
            wait_sent(stage, c)
    def settle(c, carry):
        for k in range(1, shots):
            whole_copy(k, c).wait()
        return carry

    lax.fori_loop(0, CHUNKS, settle, 0)
    store = pltpu.make_async_copy(total, total_out, load_sem.at[0])
    store.start()

    def hear(k, carry):
        square_copy(k).wait()
        return carry

    lax.fori_loop(1, team, hear, 0)
    everything = jnp.sum(squares[...], axis=0)
    cells = slabs * depth * width * lanes
    mean = jnp.sum(everything, keepdims=True) / cells + tiny_eps
    inv_out[...] = jnp.broadcast_to(1.0 / jnp.sqrt(mean), inv_out.shape)
    store.wait()


def finish(total, slowness, inverse, new_slowness, gradient):
    share = gradient.shape[1]
    first = pl.multiple_of(lax.axis_index("shot") * share, 8)
    inv = inverse[0:1]
    for d in range(total.shape[0]):
        new_slowness[d] = slowness[d] - update_rate * (total[d] * inv)
        gradient[d] = total[d, pl.ds(first, share)] * inv


def per_device(
    slowness,
    wave_prev,
    wave_now,
    memory,
    adjoint_now,
    adjoint_prev,
    wavelet,
    src_cells,
    src_signs,
    rec_cells,
    observed,
):
    depth, width, lanes = slowness.shape
    shots, slabs = lax.axis_size("shot"), lax.axis_size("slab")
    rows = width // CHUNKS
    piece = depth * rows // shots
    assert width % 96 == 0 and depth >= LINK
    assert depth * rows % shots == 0 and rows % piece == 0 and piece % 8 == 0
    receivers = rec_cells.shape[0]
    stages = 2 * STEPS - 1
    f32 = jnp.float32
    block = (depth, width, lanes)
    padded = (depth, width + 2 * PAD, lanes)
    anywhere = pl.BlockSpec(memory_space=pl.ANY)
    vmem = pl.BlockSpec(memory_space=pltpu.VMEM)
    dma = pltpu.SemaphoreType.DMA
    total, inverse = pl.pallas_call(
        functools.partial(kernel, shots, slabs),
        name="invert",
        out_shape=(
            jax.ShapeDtypeStruct(block, f32),
            jax.ShapeDtypeStruct((8, lanes), f32),
        ),
        in_specs=[anywhere] * 11,
        out_specs=(anywhere, vmem),
        scratch_shapes=[
            pltpu.VMEM(block, f32),
            pltpu.VMEM(block, f32),
            pltpu.VMEM((STEPS + 1, *padded), f32),
            pltpu.VMEM((MECH, *block), f32),
            pltpu.VMEM(block, f32),
            pltpu.VMEM(block, f32),
            pltpu.VMEM((STEPS - 1, *padded), f32),
            pltpu.VMEM((STEPS, *block), f32),
            pltpu.VMEM((STEPS, *block), f32),
            pltpu.VMEM((STEPS, *block), f32),
            pltpu.VMEM((STEPS - 1, *block), f32),
            pltpu.VMEM(block, f32),
            pltpu.VMEM(block, f32),
            pltpu.VMEM(block, f32),
            pltpu.VMEM(block, f32),
            pltpu.VMEM(block, f32),
            pltpu.VMEM((STEPS, depth * width, lanes), f32),
            pltpu.VMEM(block, f32),
            pltpu.VMEM((depth * width, receivers), jnp.bfloat16),
            pltpu.VMEM(((1 + 3 * STEPS) * lanes, receivers), jnp.bfloat16),
            pltpu.VMEM((stages, 2, LINK, width, lanes), f32),
            pltpu.VMEM(block, f32),
            pltpu.VMEM((CHUNKS, shots - 1, piece, lanes), f32),
            pltpu.VMEM(block, f32),
            pltpu.VMEM((shots * slabs, 8, lanes), f32),
            pltpu.SMEM(wavelet.shape, f32),
            pltpu.VMEM(src_cells.shape, jnp.int32),
            pltpu.VMEM(src_signs.shape, jnp.int32),
            pltpu.VMEM((1, receivers), jnp.int32),
            pltpu.VMEM(observed.shape, f32),
            dma((11,)),
            dma((stages, 2, CHUNKS)),
            dma((stages, 2, CHUNKS)),
            dma((CHUNKS, shots - 1)),
            dma((CHUNKS, shots - 1)),
            dma((CHUNKS, shots - 1)),
            dma((CHUNKS, shots - 1)),
            dma((shots * slabs - 1,)),
            dma((shots * slabs - 1,)),
        ],
        compiler_params=pltpu.CompilerParams(
            collective_id=0, has_side_effects=True, vmem_limit_bytes=60 * 2**20
        ),
    )(
        slowness,
        wave_prev,
        wave_now,
        memory,
        adjoint_now,
        adjoint_prev,
        wavelet,
        src_cells,
        src_signs,
        rec_cells.reshape(1, receivers),
        observed,
    )
    share = width // shots
    new_slowness, gradient = pl.pallas_call(
        finish,
        name="finish",
        out_shape=(
            jax.ShapeDtypeStruct(block, f32),
            jax.ShapeDtypeStruct((depth, share, lanes), f32),
        ),
        in_specs=[vmem] * 3,
        out_specs=(vmem, vmem),
        compiler_params=pltpu.CompilerParams(vmem_limit_bytes=60 * 2**20),
    )(total, slowness, inverse)
    return (new_slowness, gradient)


def solution(mesh):
    in_specs = (
        P(("groups", "slab"), None, None),
        P(("groups", "shot"), "slab", None, None),
        P(("groups", "shot"), "slab", None, None),
        P(("groups", "shot"), None, "slab", None, None),
        P(("groups", "shot"), "slab", None, None),
        P(("groups", "shot"), "slab", None, None),
        P(),
        P(("groups", "shot"), None),
        P(("groups", "shot"), None),
        P("groups"),
        P(("groups", "shot"), None, None),
    )
    out_specs = (P(("groups", "slab"), None, None), P(("groups", "slab"), "shot", None))
    return jax.shard_map(
        per_device, mesh=mesh, in_specs=in_specs, out_specs=out_specs, check_vma=False
    )
```

```python
import functools

import jax
import jax.numpy as jnp
from jax import lax
from jax.experimental import pallas as pl
from jax.experimental.pallas import tpu as pltpu
from jax.sharding import PartitionSpec as P

STEPS = 4
MECH = 3
LINK = 2
PAD = 8
CHUNKS = 3
SUB = 32

center_coef = -2.5
near_coef = 4.0 / 3.0
far_coef = -1.0 / 12.0
courant = 0.14
relax_decay = (0.3, 0.7, 0.95)
relax_weight = (0.3, 0.2, 0.1)
update_rate = 0.05
tiny_eps = 1e-06

lag_weight = tuple(
    sum(w * a**j for w, a in zip(relax_weight, relax_decay)) for j in range(STEPS - 1)
)

MESH = pl.DeviceIdType.MESH


def contract_lanes(a, b):
    return lax.dot_general(a, b, (((1,), (1,)), ((), ())), preferred_element_type=jnp.float32)


def kernel(
    shots,
    slabs,
    slowness_in,
    prev_in,
    now_in,
    memory_in,
    adj_now_in,
    adj_prev_in,
    wavelet_in,
    src_cells_in,
    src_signs_in,
    rec_cells_in,
    observed_in,
    total_out,
    inv_out,
    slow,
    older,
    field,
    relax,
    adj_now,
    adj_prev,
    drive,
    united,
    saved,
    fading,
    curves,
    pushes,
    accum,
    scaled,
    factor,
    count,
    seen,
    source,
    hot_rows,
    pieces,
    halo,
    grad,
    parts,
    total,
    squares,
    sums,
    wavelet,
    src_cells,
    src_signs,
    rec_cells,
    observed,
    load_sem,
    halo_send,
    halo_recv,
    part_send,
    part_recv,
    whole_send,
    whole_recv,
    square_send,
    square_recv,
    sum_send,
    sum_recv,
):
    depth, width, lanes = slow.shape
    rows = width // CHUNKS
    stages = 2 * STEPS - 1
    me = lax.axis_index("slab")
    shot = lax.axis_index("shot")

    loads = [
        pltpu.make_async_copy(now_in.at[0], field.at[0, :, PAD : PAD + width], load_sem.at[0]),
        pltpu.make_async_copy(slowness_in, slow, load_sem.at[1]),
        pltpu.make_async_copy(memory_in.at[0], relax, load_sem.at[2]),
        pltpu.make_async_copy(prev_in.at[0], older, load_sem.at[3]),
        pltpu.make_async_copy(adj_now_in.at[0], adj_now, load_sem.at[4]),
        pltpu.make_async_copy(adj_prev_in.at[0], adj_prev, load_sem.at[5]),
        pltpu.make_async_copy(wavelet_in, wavelet, load_sem.at[6]),
        pltpu.make_async_copy(src_cells_in, src_cells, load_sem.at[7]),
        pltpu.make_async_copy(src_signs_in, src_signs, load_sem.at[8]),
        pltpu.make_async_copy(rec_cells_in, rec_cells, load_sem.at[9]),
        pltpu.make_async_copy(observed_in, observed, load_sem.at[10]),
    ]
    barrier = pltpu.get_barrier_semaphore()
    for k in range(1, slabs):
        pl.semaphore_signal(
            barrier, inc=1, device_id={"slab": lax.rem(me + k, slabs)}, device_id_type=MESH
        )
    for k in range(1, shots):
        pl.semaphore_signal(
            barrier, inc=1, device_id={"shot": lax.rem(shot + k, shots)}, device_id_type=MESH
        )
    for copy in loads:
        copy.start()
    pl.semaphore_wait(barrier, slabs - 1 + shots - 1)

    def outgoing(stage, side, c):
        first = depth - LINK if side == 0 else 0
        planes = pl.ds(first, LINK)
        start = pl.multiple_of(c * rows, 8)
        if stage == 0:
            src = now_in.at[0, planes, pl.ds(start, rows)]
        elif stage < STEPS:
            src = field.at[stage, planes, pl.ds(start + PAD, rows)]
        else:
            src = drive.at[stage - STEPS, planes, pl.ds(start + PAD, rows)]
        target = me + 1 if side == 0 else me - 1
        return pltpu.make_async_remote_copy(
            src_ref=src,
            dst_ref=halo.at[stage, side, :, pl.ds(start, rows)],
            send_sem=halo_send.at[stage, side, c],
            recv_sem=halo_recv.at[stage, side, c],
            device_id={"slab": target},
            device_id_type=MESH,
        )

    has_up = me < slabs - 1
    has_down = me > 0

    def send_halo(stage, c):
        @pl.when(has_up)
        def _():
            outgoing(stage, 0, c).start()

        @pl.when(has_down)
        def _():
            outgoing(stage, 1, c).start()

    def wait_sent(stage, c):
        @pl.when(has_up)
        def _():
            outgoing(stage, 0, c).wait_send()

        @pl.when(has_down)
        def _():
            outgoing(stage, 1, c).wait_send()

    def wait_halo(stage, c):
        @pl.when(has_down)
        def _():
            outgoing(stage, 0, c).wait_recv()

        @pl.when(has_up)
        def _():
            outgoing(stage, 1, c).wait_recv()

    for c in range(CHUNKS):
        send_halo(0, c)

    @pl.when(jnp.logical_not(has_down))
    def _():
        halo[:, 0] = jnp.zeros((stages, LINK, width, lanes), jnp.float32)

    @pl.when(jnp.logical_not(has_up))
    def _():
        halo[:, 1] = jnp.zeros((stages, LINK, width, lanes), jnp.float32)

    edge = jnp.zeros((depth, PAD, lanes), jnp.float32)
    for n in range(STEPS):
        field[n, :, :PAD] = edge
        field[n, :, PAD + width :] = edge
    for n in range(STEPS - 1):
        drive[n, :, :PAD] = edge
        drive[n, :, PAD + width :] = edge

    def one_hot(index, height):
        at = lax.broadcasted_iota(jnp.int32, (height, index.shape[1]), 0)
        return jnp.where(at == index, 1.0, 0.0)

    first_row = me * (depth * width)
    for k in range(6, 11):
        loads[k].wait()
    src = src_cells[...]
    src_row = lax.div(src, lanes)
    src_lane = src - src_row * lanes
    src_at = (one_hot(src_lane, lanes) * src_signs[...].astype(jnp.float32)).astype(jnp.bfloat16)
    src_rows = one_hot(src_row - first_row, depth * width).astype(jnp.bfloat16)
    source[...] = contract_lanes(src_rows, src_at).reshape(depth, width, lanes)

    def place_receivers():
        rec = rec_cells[...]
        rec_row = lax.div(rec, lanes)
        rec_lane = rec - rec_row * lanes
        at_lane = one_hot(rec_lane, lanes)
        pieces[0:lanes] = at_lane.astype(jnp.bfloat16)
        for n in range(STEPS):
            rest = at_lane * observed[0, n : n + 1, :]
            for k in range(3):
                part = rest.astype(jnp.bfloat16)
                begin = (1 + 3 * n + k) * lanes
                pieces[begin : begin + lanes] = part
                rest = rest - part.astype(jnp.float32)
        hot_rows[...] = one_hot(rec_row - first_row, depth * width).astype(jnp.bfloat16)
        count[...] = contract_lanes(hot_rows[...], pieces[0:lanes]).reshape(depth, width, lanes)

    def place_observed(n, part, parts_of):
        height = depth * width // parts_of
        at = pl.ds(pl.multiple_of(part * height, 16), height)
        begin = (1 + 3 * n) * lanes
        got = contract_lanes(hot_rows[at], pieces[begin : begin + 3 * lanes])
        seen[n, at] = (got[:, 2 * lanes :] + got[:, lanes : 2 * lanes]) + got[:, :lanes]

    loads[1].wait()
    for d in range(depth):
        s = slow[d]
        held = courant / (s * s)
        scaled[d] = held
        factor[d] = (-2.0 * held) / s
    loads[2].wait()

    def fade(k, carry):
        at = pl.ds(pl.multiple_of(k * SUB, 8), SUB)
        for d in range(depth):
            held = [relax[m, d, at] for m in range(MECH)]
            for n in range(STEPS):
                fading[n, d, at] = (held[0] + held[1]) + held[2]
                held = [relax_decay[m] * held[m] for m in range(MECH)]
        return carry

    lax.fori_loop(0, width // SUB, fade, 0)
    for k in (0, 3, 4, 5):
        loads[k].wait()
    place_receivers()
    place_observed(STEPS - 1, 0, 1)

    lane = lax.broadcasted_iota(jnp.int32, (8, lanes), 1)[:1]
    left_1 = jnp.where(lane >= 1, near_coef, 0.0)
    left_2 = jnp.where(lane >= 2, far_coef, 0.0)
    right_1 = jnp.where(lane < lanes - 1, near_coef, 0.0)
    right_2 = jnp.where(lane < lanes - 2, far_coef, 0.0)

    def laplace(ref, n, stage, r):
        def rows_at(d, shift):
            return ref[n, d, pl.ds(r + PAD + shift, SUB)]

        low = [halo[stage, 0, k, pl.ds(r, SUB)] for k in range(LINK)]
        mids = [rows_at(d, 0) for d in range(depth)]
        high = [halo[stage, 1, k, pl.ds(r, SUB)] for k in range(LINK)]
        planes = low + mids + high
        curved = []
        for d in range(depth):
            mid = mids[d]
            near = (planes[d + 1] + planes[d + 3]) + (rows_at(d, -1) + rows_at(d, 1))
            far = (planes[d] + planes[d + 4]) + (rows_at(d, -2) + rows_at(d, 2))
            along = (
                left_1 * pltpu.roll(mid, 1, 1)
                + right_1 * pltpu.roll(mid, lanes - 1, 1)
                + left_2 * pltpu.roll(mid, 2, 1)
                + right_2 * pltpu.roll(mid, lanes - 2, 1)
            )
            curved.append(
                (3.0 * center_coef) * mid + near_coef * near + far_coef * far + along
            )
        return curved, mids

    def blocks(c, body):
        for k in range(rows // SUB):
            body(pl.multiple_of(c * rows + k * SUB, 8))

    def adjoint_part(level, d, r, back, begin_accum):
        at = pl.ds(r, SUB)
        up = back + (
            count[d, at] * field[level + 1, d, pl.ds(r + PAD, SUB)] - seen[level, pl.ds(d * width + r, SUB)]
        )
        term = up * saved[level, d, at]
        term = term if begin_accum else accum[d, at] + term
        if level == 0:
            grad[d, at] = term * factor[d, at]
            return
        accum[d, at] = term
        united[level, d, at] = up
        pushed = scaled[d, at] * up
        out = pushed
        if level == STEPS - 2:
            pushes[d, at] = pushed
            out = pushed - lag_weight[0] * drive[0, d, pl.ds(r + PAD, SUB)]
        elif level == STEPS - 3:
            out = (pushed - lag_weight[0] * pushes[d, at]) - lag_weight[1] * drive[
                0, d, pl.ds(r + PAD, SUB)
            ]
        drive[STEPS - 1 - level, d, pl.ds(r + PAD, SUB)] = out

    def forward_stage(n):
        amount = wavelet[n]

        def chunk(c, carry):
            wait_halo(n, c)
            if n > 0:
                wait_sent(n - 1, c)

            def body(r):
                at = pl.ds(r, SUB)
                inner = pl.ds(r + PAD, SUB)
                curved, mids = laplace(field, n, n, r)
                for d in range(depth):
                    accel = curved[d] + fading[n, d, at]
                    for m in range(n):
                        accel = accel - lag_weight[n - 1 - m] * curves[m, d, at]
                    before = older[d, at] if n == 0 else field[n - 1, d, inner]
                    newer = (2.0 * mids[d] - before) + scaled[d, at] * accel
                    newer = newer + amount * source[d, at]
                    saved[n, d, at] = accel
                    field[n + 1, d, inner] = newer
                    if n < STEPS - 1:
                        curves[n, d, at] = curved[d]
                    else:
                        adjoint_part(n, d, r, adj_now[d, at], True)

            blocks(c, body)
            send_halo(n + 1, c)
            if n < STEPS - 1:
                place_observed(STEPS - 2 - n, c, CHUNKS)
            return carry

        lax.fori_loop(0, CHUNKS, chunk, 0)

    piece = depth * rows // shots

    def spot(owner, c):
        begin = owner * piece
        return begin // rows, pl.multiple_of(c * rows + begin % rows, 8)

    def part_copy(k, c):
        target = lax.rem(shot + k, shots)
        d, r = spot(target, c)
        return pltpu.make_async_remote_copy(
            src_ref=grad.at[d, pl.ds(r, piece)],
            dst_ref=parts.at[c, k - 1],
            send_sem=part_send.at[c, k - 1],
            recv_sem=part_recv.at[c, k - 1],
            device_id={"shot": target},
            device_id_type=MESH,
        )

    def whole_copy(k, c):
        target = lax.rem(shot + k, shots)
        d, r = spot(shot, c)
        return pltpu.make_async_remote_copy(
            src_ref=total.at[d, pl.ds(r, piece)],
            dst_ref=total.at[d, pl.ds(r, piece)],
            send_sem=whole_send.at[c, k - 1],
            recv_sem=whole_recv.at[c, k - 1],
            device_id={"shot": target},
            device_id_type=MESH,
        )

    def reduce_chunk(c):
        d, r = spot(shot, c)
        held = grad[d, pl.ds(r, piece)]
        for k in range(1, shots):
            part_copy(k, c).wait_recv()
            held = held + parts[c, k - 1]
        total[d, pl.ds(r, piece)] = held
        for k in range(1, shots):
            whole_copy(k, c).start()

    def backward_stage(level):
        stage = 2 * STEPS - 2 - level

        def chunk(c, carry):
            wait_halo(stage, c)
            wait_sent(stage - 1, c)

            def body(r):
                at = pl.ds(r, SUB)
                curved, _ = laplace(drive, stage - STEPS, stage, r)
                for d in range(depth):
                    after = united[level + 1, d, at]
                    if level == STEPS - 2:
                        base = adj_prev[d, at]
                    else:
                        base = -united[level + 2, d, at]
                    adjoint_part(level, d, r, (base + 2.0 * after) + curved[d], False)

            blocks(c, body)
            if level > 0:
                send_halo(stage + 1, c)
            else:
                for k in range(1, shots):
                    part_copy(k, c).start()

                @pl.when(c >= 2)
                def _():
                    reduce_chunk(c - 2)

            return carry

        lax.fori_loop(0, CHUNKS, chunk, 0)

    for n in range(STEPS):
        forward_stage(n)
    for level in reversed(range(STEPS - 1)):
        backward_stage(level)
    for c in range(CHUNKS - 2, CHUNKS):
        reduce_chunk(c)

    summed = jnp.zeros((8, lanes), jnp.float32)
    for c in range(CHUNKS):
        d, r = spot(shot, c)
        held = total[d, pl.ds(r, piece)]
        summed = summed + jnp.sum((held * held).reshape(piece // 8, 8, lanes), axis=0)
    squares[me] = summed

    def square_copy(k):
        return pltpu.make_async_remote_copy(
            src_ref=squares.at[me],
            dst_ref=squares.at[me],
            send_sem=square_send.at[k - 1],
            recv_sem=square_recv.at[k - 1],
            device_id={"slab": lax.rem(me + k, slabs)},
            device_id_type=MESH,
        )

    def shot_copy(k):
        return pltpu.make_async_remote_copy(
            src_ref=sums.at[shot],
            dst_ref=sums.at[shot],
            send_sem=sum_send.at[k - 1],
            recv_sem=sum_recv.at[k - 1],
            device_id={"shot": lax.rem(shot + k, shots)},
            device_id_type=MESH,
        )

    for k in range(1, slabs):
        square_copy(k).start()

    def settle_parts(c, carry):
        wait_sent(stages - 1, c)
        for k in range(1, shots):
            part_copy(k, c).wait_send()
        return carry

    lax.fori_loop(0, CHUNKS, settle_parts, 0)
    for k in range(1, slabs):
        square_copy(k).wait_recv()
    everything = squares[0]
    for k in range(1, slabs):
        everything = everything + squares[k]
    sums[shot] = everything
    for k in range(1, shots):
        shot_copy(k).start()

    def settle(c, carry):
        for k in range(1, shots):
            whole_copy(k, c).wait()
        return carry

    lax.fori_loop(0, CHUNKS, settle, 0)
    store = pltpu.make_async_copy(total, total_out, load_sem.at[0])
    store.start()
    for k in range(1, slabs):
        square_copy(k).wait_send()
    for k in range(1, shots):
        shot_copy(k).wait()
    everything = sums[0]
    for k in range(1, shots):
        everything = everything + sums[k]
    cells = slabs * depth * width * lanes
    mean = jnp.sum(everything, keepdims=True) / cells + tiny_eps
    inv_out[...] = jnp.broadcast_to(1.0 / jnp.sqrt(mean), inv_out.shape)
    store.wait()


def finish(total, slowness, inverse, new_slowness, gradient):
    share = gradient.shape[1]
    first = pl.multiple_of(lax.axis_index("shot") * share, 8)
    inv = inverse[0:1]
    for d in range(total.shape[0]):
        new_slowness[d] = slowness[d] - update_rate * (total[d] * inv)
        gradient[d] = total[d, pl.ds(first, share)] * inv


def per_device(
    slowness,
    wave_prev,
    wave_now,
    memory,
    adjoint_now,
    adjoint_prev,
    wavelet,
    src_cells,
    src_signs,
    rec_cells,
    observed,
):
    depth, width, lanes = slowness.shape
    shots, slabs = lax.axis_size("shot"), lax.axis_size("slab")
    rows = width // CHUNKS
    piece = depth * rows // shots
    assert width % CHUNKS == 0 and rows % SUB == 0 and depth >= LINK
    assert depth * rows % shots == 0 and rows % piece == 0 and piece % 8 == 0
    receivers = rec_cells.shape[0]
    stages = 2 * STEPS - 1
    f32 = jnp.float32
    block = (depth, width, lanes)
    padded = (depth, width + 2 * PAD, lanes)
    anywhere = pl.BlockSpec(memory_space=pl.ANY)
    vmem = pl.BlockSpec(memory_space=pltpu.VMEM)
    dma = pltpu.SemaphoreType.DMA
    total, inverse = pl.pallas_call(
        functools.partial(kernel, shots, slabs),
        name="invert",
        out_shape=(
            jax.ShapeDtypeStruct(block, f32),
            jax.ShapeDtypeStruct((8, lanes), f32),
        ),
        in_specs=[anywhere] * 11,
        out_specs=(anywhere, vmem),
        scratch_shapes=[
            pltpu.VMEM(block, f32),
            pltpu.VMEM(block, f32),
            pltpu.VMEM((STEPS + 1, *padded), f32),
            pltpu.VMEM((MECH, *block), f32),
            pltpu.VMEM(block, f32),
            pltpu.VMEM(block, f32),
            pltpu.VMEM((STEPS - 1, *padded), f32),
            pltpu.VMEM((STEPS, *block), f32),
            pltpu.VMEM((STEPS, *block), f32),
            pltpu.VMEM((STEPS, *block), f32),
            pltpu.VMEM((STEPS - 1, *block), f32),
            pltpu.VMEM(block, f32),
            pltpu.VMEM(block, f32),
            pltpu.VMEM(block, f32),
            pltpu.VMEM(block, f32),
            pltpu.VMEM(block, f32),
            pltpu.VMEM((STEPS, depth * width, lanes), f32),
            pltpu.VMEM(block, f32),
            pltpu.VMEM((depth * width, receivers), jnp.bfloat16),
            pltpu.VMEM(((1 + 3 * STEPS) * lanes, receivers), jnp.bfloat16),
            pltpu.VMEM((stages, 2, LINK, width, lanes), f32),
            pltpu.VMEM(block, f32),
            pltpu.VMEM((CHUNKS, shots - 1, piece, lanes), f32),
            pltpu.VMEM(block, f32),
            pltpu.VMEM((slabs, 8, lanes), f32),
            pltpu.VMEM((shots, 8, lanes), f32),
            pltpu.SMEM(wavelet.shape, f32),
            pltpu.VMEM(src_cells.shape, jnp.int32),
            pltpu.VMEM(src_signs.shape, jnp.int32),
            pltpu.VMEM((1, receivers), jnp.int32),
            pltpu.VMEM(observed.shape, f32),
            dma((11,)),
            dma((stages, 2, CHUNKS)),
            dma((stages, 2, CHUNKS)),
            dma((CHUNKS, shots - 1)),
            dma((CHUNKS, shots - 1)),
            dma((CHUNKS, shots - 1)),
            dma((CHUNKS, shots - 1)),
            dma((slabs - 1,)),
            dma((slabs - 1,)),
            dma((shots - 1,)),
            dma((shots - 1,)),
        ],
        compiler_params=pltpu.CompilerParams(
            collective_id=0, has_side_effects=True, vmem_limit_bytes=60 * 2**20
        ),
    )(
        slowness,
        wave_prev,
        wave_now,
        memory,
        adjoint_now,
        adjoint_prev,
        wavelet,
        src_cells,
        src_signs,
        rec_cells.reshape(1, receivers),
        observed,
    )
    share = width // shots
    new_slowness, gradient = pl.pallas_call(
        finish,
        name="finish",
        out_shape=(
            jax.ShapeDtypeStruct(block, f32),
            jax.ShapeDtypeStruct((depth, share, lanes), f32),
        ),
        in_specs=[vmem] * 3,
        out_specs=(vmem, vmem),
        compiler_params=pltpu.CompilerParams(vmem_limit_bytes=60 * 2**20),
    )(total, slowness, inverse)
    return (new_slowness, gradient)


def solution(mesh):
    in_specs = (
        P(("groups", "slab"), None, None),
        P(("groups", "shot"), "slab", None, None),
        P(("groups", "shot"), "slab", None, None),
        P(("groups", "shot"), None, "slab", None, None),
        P(("groups", "shot"), "slab", None, None),
        P(("groups", "shot"), "slab", None, None),
        P(),
        P(("groups", "shot"), None),
        P(("groups", "shot"), None),
        P("groups"),
        P(("groups", "shot"), None, None),
    )
    out_specs = (P(("groups", "slab"), None, None), P(("groups", "slab"), "shot", None))
    return jax.shard_map(
        per_device, mesh=mesh, in_specs=in_specs, out_specs=out_specs, check_vma=False
    )
```
